768 devices in a mesh: tm: 96 (over x, z, y_lo), space: 8 (over y_hi, core).
Axes of the slice: x: 4, y: 8 (y_hi: 4, y_lo: 2; y = y_hi * 2 + y_lo), z: 12, core: 2. Of those that a mesh axis runs over, the one named last changes fastest.
Arguments:
- state_field: float32 [96, 64, 12, 128], P('tm', 'space'), may hold values from -6 to 6
- adjoint: float32 [96, 64, 12, 128], P('tm', 'space'), may hold values from -6 to 6
- target: float32 [96, 64, 12, 128], P('tm', 'space'), may hold values from -4 to 4
- conductivity: float32 [64, 12, 128], P('space'), may hold values from 0.2 to 2
Outputs:
- residual_state: float32 [96, 64, 12, 128], P('tm', 'space')
- residual_adjoint: float32 [96, 64, 12, 128], P('tm', 'space')
- spectral_correction: float32 [4, 96, 64, 1536], P(None, None, 'space', 'tm')
The draws below stay inside these ranges and needn't reach their ends.
All inputs are finite; a program needn't handle non-finite values.
Results may differ from the reference program's by a relative error of at most 0.00013.
Values sent between devices are 32-bit elements; how exact they have to be, the bound alone decides.
A program may use at most 32 MiB of HBM per device.

```python
import math
import jax
import jax.numpy as jnp

NX = 12
NY = 128
NT = 96
NZ = 64


def draw_target(key, part):
    shape_all = (NT, NZ, NX, NY)
    return jnp.clip(jax.random.normal(key, shape_all, jnp.float32), -4.0, 4.0)


def levels(own_key, dims, pieces, smallest, high):
    loudness, own = 1.0, jax.random.fold_in(own_key, 6)
    for axis_at, shards_of in pieces:
        heights = jnp.exp(jax.random.uniform(jax.random.fold_in(own, axis_at), (shards_of,), jnp.float32, smallest / len(pieces), high / len(pieces)))
        loudness = loudness * jnp.repeat(heights, dims[axis_at] // shards_of).reshape([-1 if axis == axis_at else 1 for axis in range(len(dims))])
    return loudness


def gaussian(own_key, extent, spread, bound, cuts=(), kind=jnp.bfloat16):
    result = spread * jax.random.normal(own_key, extent, jnp.float32)
    if cuts:
        result = result * levels(own_key, extent, cuts, -0.22, 0.18)
    return jnp.clip(result, -bound, bound).astype(kind)


def setup_inputs(seed: int = 0) -> dict:
    seeds = jax.random.split(jax.random.key(seed), 5)
    return {
        "state_field": gaussian(seeds[0], (NT, NZ, NX, NY), 1.0, 6.0, ((0, 96), (1, 8)), jnp.float32),
        "adjoint": gaussian(seeds[1], (NT, NZ, NX, NY), 1.0, 6.0, ((0, 96), (1, 8)), jnp.float32),
        "target": draw_target(jax.random.fold_in(seeds[4], 71), 0),
        "conductivity": jnp.clip(jnp.exp(math.log(2.0) - 2.3025851 * jax.random.uniform(seeds[3], (NZ, NX, NY), jnp.float32) ** levels(seeds[3], (NZ, NX, NY), ((0, 8),), -0.2, 0.2)), 0.2, 2.0),
    }


diffusion = 0.05
control_cost = 0.2
tracking = 0.5

def plane_sum(values_in):
    zero_row = jnp.zeros_like(values_in[..., :1, :])
    along_x = jnp.concatenate([values_in[..., 1:, :], zero_row], axis=-2) + jnp.concatenate([zero_row, values_in[..., :-1, :]], axis=-2)
    zero_col = jnp.zeros_like(values_in[..., :1])
    along_y = jnp.concatenate([values_in[..., 1:], zero_col], axis=-1) + jnp.concatenate([zero_col, values_in[..., :-1]], axis=-1)
    return along_x + along_y

def around_sum(values_in):
    padded = jnp.pad(values_in, ((0, 0), (1, 1), (0, 0), (0, 0)))
    return padded[:, :-2] + padded[:, 2:] + plane_sum(values_in)

def reference(state_field, adjoint, target, conductivity):
    step_count = state_field.shape[0]
    depth = state_field.shape[1]
    plane_cells = state_field.shape[2] * state_field.shape[3]
    weighted = conductivity[None] * adjoint
    diffused_state = conductivity[None] * (6.0 * state_field - around_sum(state_field))
    diffused_adjoint = 6.0 * weighted - around_sum(weighted)
    residual_state = state_field - jnp.roll(state_field, 1, axis=0) + diffusion * diffused_state - control_cost * adjoint
    residual_adjoint = adjoint - jnp.roll(adjoint, -1, axis=0) + diffusion * diffused_adjoint + tracking * (state_field - target)
    scale_norm = 1.0 / math.sqrt(step_count)
    spec_state = jnp.fft.fft(residual_state.reshape(step_count, depth, plane_cells), axis=0) * scale_norm
    spec_adjoint = jnp.fft.fft(residual_adjoint.reshape(step_count, depth, plane_cells), axis=0) * scale_norm
    state_real = jnp.real(spec_state).astype(jnp.float32)
    state_imag = jnp.imag(spec_state).astype(jnp.float32)
    adjoint_real = jnp.real(spec_adjoint).astype(jnp.float32)
    adjoint_imag = jnp.imag(spec_adjoint).astype(jnp.float32)
    step_index = jnp.arange(step_count, dtype=jnp.int32)
    unit_angle = step_index.astype(jnp.float32) * (2.0 * math.pi / step_count)
    cosine_step = jnp.cos(unit_angle)[:, None, None]
    sine_step = jnp.sin(unit_angle)[:, None, None]
    diagonal_term = 1.0 + diffusion * 6.0 * conductivity.reshape(1, depth, plane_cells) - cosine_step
    determinant = diagonal_term * diagonal_term + sine_step * sine_step + control_cost * tracking
    fix_state_real = (diagonal_term * state_real + sine_step * state_imag + control_cost * adjoint_real) / determinant
    fix_state_imag = (diagonal_term * state_imag - sine_step * state_real + control_cost * adjoint_imag) / determinant
    fix_adjoint_real = (diagonal_term * adjoint_real - sine_step * adjoint_imag - tracking * state_real) / determinant
    fix_adjoint_imag = (diagonal_term * adjoint_imag + sine_step * adjoint_real - tracking * state_imag) / determinant
    spectral_correction = jnp.stack([fix_state_real, fix_state_imag, fix_adjoint_real, fix_adjoint_imag])
    return (residual_state, residual_adjoint, spectral_correction)
```

```python
import functools
import math

import jax
import jax.numpy as jnp
import numpy as np
from jax import lax
from jax.experimental import pallas as pl
from jax.experimental.pallas import tpu as pltpu
from jax.sharding import PartitionSpec as P

diffusion = 0.05
control_cost = 0.2
tracking = 0.5

STEPS = 96
ROWS = 12
OWNERS = 8
BLOCK = 16
LANES = 128


def dft_table():
    times = np.arange(STEPS)
    angles = (np.outer(times, times) % STEPS) * (2.0 * math.pi / STEPS)
    table = np.zeros((OWNERS, ROWS, 2, 4, LANES))
    for r in range(OWNERS):
        for j in range(ROWS):
            for field in range(2):
                table[r, j, field, 2 * field, :STEPS] = np.cos(angles[8 * j + r])
                table[r, j, field, 2 * field + 1, :STEPS] = -np.sin(angles[8 * j + r])
    table = table.reshape(2 * STEPS, 4 * LANES) / math.sqrt(STEPS)
    trig = np.zeros((8, LANES))
    trig[0, :STEPS] = np.cos(times * (2.0 * math.pi / STEPS))
    trig[1, :STEPS] = np.sin(times * (2.0 * math.pi / STEPS))
    return table.astype(np.float32), trig.astype(np.float32)


def swap_blocks(tile):
    row = lax.broadcasted_iota(jnp.int32, (8, LANES), 0)
    block = lax.broadcasted_iota(jnp.int32, (8, LANES), 1) // BLOCK
    for bit in (1, 2, 4):
        row_set = (row & bit) != 0
        block_set = (block & bit) != 0
        up = pltpu.roll(pltpu.roll(tile, 8 - bit, 0), BLOCK * bit, 1)
        if bit == 4:
            tile = jnp.where(row_set == block_set, tile, up)
        else:
            down = pltpu.roll(pltpu.roll(tile, bit, 0), LANES - BLOCK * bit, 1)
            tile = jnp.where(row_set == block_set, tile, jnp.where(block_set, up, down))
    return tile


def kernel(
    s_hbm, p_hbm, target_hbm, cond_hbm, table_hbm, trig_ref,
    rs_ref, rp_ref, spec_ref,
    s_pad, p_v, w_pad, target_v, cond_v, table_v,
    s_prev, p_next, edge_low, edge_high, from_low, from_high,
    send_a, recv_a, send_b, recv_b, cond_rows,
    load_sem, near_send, near_recv, a_send, a_recv, b_send, b_recv,
):
    tm = lax.axis_index("tm")
    space = lax.axis_index("space")
    group = lax.div(tm, OWNERS)
    rank = lax.rem(tm, OWNERS)
    later = lax.rem(tm + 1, STEPS)
    earlier = lax.rem(tm + STEPS - 1, STEPS)
    above = lax.rem(space + 1, 8)
    below = lax.rem(space + 7, 8)

    loads = [
        pltpu.make_async_copy(source, target, load_sem.at[i])
        for i, (source, target) in enumerate(
            (
                (s_hbm, s_pad.at[pl.ds(1, ROWS)]),
                (p_hbm, p_v),
                (cond_hbm, cond_v),
                (target_hbm, target_v),
                (table_hbm, table_v),
            )
        )
    ]
    for load in loads:
        load.start()

    barrier = pltpu.get_barrier_semaphore()
    a_peers = [lax.rem(group + k, ROWS) for k in range(1, ROWS)]
    b_peers = [lax.rem(rank + k, OWNERS) for k in range(1, OWNERS)]
    for where in (
        [{"tm": later}, {"tm": earlier}, {"space": above}, {"space": below}]
        + [{"tm": peer * OWNERS + rank} for peer in a_peers]
        + [{"tm": group * OWNERS + peer} for peer in b_peers]
    ):
        pl.semaphore_signal(barrier, 1, device_id=where, device_id_type=pl.DeviceIdType.MESH)

    zero = jnp.zeros((8, LANES), jnp.float32)
    for padded in (s_pad, w_pad):
        padded[0] = zero
        padded[ROWS + 1] = zero
    for load in loads[:3]:
        load.wait()
    for x in range(ROWS):
        w_pad[x + 1] = cond_v[x] * p_v[x]
    for edge, z in ((edge_low, 0), (edge_high, 7)):
        edge[0:ROWS] = s_pad[1 : ROWS + 1, z, :]
        edge[ROWS : 2 * ROWS] = w_pad[1 : ROWS + 1, z, :]

    pl.semaphore_wait(barrier, 4 + ROWS - 1 + OWNERS - 1)

    def send(source, target, send_sem, recv_sem, where):
        copy = pltpu.make_async_remote_copy(
            src_ref=source, dst_ref=target, send_sem=send_sem, recv_sem=recv_sem,
            device_id=where, device_id_type=pl.DeviceIdType.MESH,
        )
        copy.start()
        return copy

    near = [
        send(s_pad.at[pl.ds(1, ROWS)], s_prev, near_send.at[0], near_recv.at[0], {"tm": later}),
        send(p_v, p_next, near_send.at[1], near_recv.at[1], {"tm": earlier}),
        send(edge_low, from_high, near_send.at[2], near_recv.at[2], {"space": below}),
        send(edge_high, from_low, near_send.at[3], near_recv.at[3], {"space": above}),
    ]

    cond_rows[...] = swap_blocks(cond_v[group])
    own_cond = jnp.broadcast_to(cond_rows[pl.ds(rank, 1)], (LANES, LANES)).T

    row = lax.broadcasted_iota(jnp.int32, (8, LANES), 0)
    lane = lax.broadcasted_iota(jnp.int32, (8, LANES), 1)
    loads[3].wait()
    for copy in near:
        copy.wait_recv()

    def around(padded, x, low, high):
        centre = padded[x + 1]
        low = jnp.broadcast_to(jnp.where(space == 0, 0.0, low), (8, LANES))
        high = jnp.broadcast_to(jnp.where(space == 7, 0.0, high), (8, LANES))
        z_low = jnp.where(row == 0, low, pltpu.roll(centre, 1, 0))
        z_high = jnp.where(row == 7, high, pltpu.roll(centre, 7, 0))
        y_low = jnp.where(lane == 0, 0.0, pltpu.roll(centre, 1, 1))
        y_high = jnp.where(lane == LANES - 1, 0.0, pltpu.roll(centre, LANES - 1, 1))
        return (z_low + z_high) + (padded[x] + padded[x + 2]) + (y_low + y_high)

    for x in range(ROWS):
        s, p, w, cond = s_pad[x + 1], p_v[x], w_pad[x + 1], cond_v[x]
        around_s = around(s_pad, x, from_low[x : x + 1], from_high[x : x + 1])
        around_w = around(
            w_pad, x, from_low[ROWS + x : ROWS + x + 1], from_high[ROWS + x : ROWS + x + 1]
        )
        rs = s - s_prev[x] + diffusion * (cond * (6.0 * s - around_s)) - control_cost * p
        rp = p - p_next[x] + diffusion * (6.0 * w - around_w) + tracking * (s - target_v[x])
        rs_ref[x] = rs
        rp_ref[x] = rp
        send_a[x, 0] = swap_blocks(rs)
        send_a[x, 1] = swap_blocks(rp)

    copies_a = [
        send(send_a.at[peer], recv_a.at[group], a_send.at[k], a_recv.at[k],
             {"tm": peer * OWNERS + rank})
        for k, peer in enumerate(a_peers)
    ]
    recv_a[group] = send_a[group]
    for copy in copies_a:
        copy.wait_recv()
    for block in range(OWNERS):
        for part in range(3):
            send_b[block, 8 * part : 8 * part + 8] = recv_a[
                4 * part : 4 * part + 4, :, block, :
            ].reshape(8, LANES)
    copies_b = [
        send(send_b.at[peer], recv_b.at[rank], b_send.at[k], b_recv.at[k],
             {"tm": group * OWNERS + peer})
        for k, peer in enumerate(b_peers)
    ]
    recv_b[rank] = send_b[rank]
    loads[4].wait()
    for copy in copies_b:
        copy.wait_recv()

    spectra = lax.dot_general(
        recv_b[...].reshape(2 * STEPS, LANES), table_v[...], (((0,), (0,)), ((), ())),
        precision=lax.Precision.HIGHEST, preferred_element_type=jnp.float32,
    )
    state_real, state_imag, adjoint_real, adjoint_imag = (
        spectra[:, LANES * i : LANES * (i + 1)] for i in range(4)
    )
    cosine, sine = trig_ref[0:1], trig_ref[1:2]
    diagonal = 1.0 + diffusion * 6.0 * own_cond - cosine
    scale = 1.0 / (diagonal * diagonal + sine * sine + control_cost * tracking)
    fixes = (
        diagonal * state_real + sine * state_imag + control_cost * adjoint_real,
        diagonal * state_imag - sine * state_real + control_cost * adjoint_imag,
        diagonal * adjoint_real - sine * adjoint_imag - tracking * state_real,
        diagonal * adjoint_imag + sine * adjoint_real - tracking * state_imag,
    )
    for i, fix in enumerate(fixes):
        spec_ref[i] = (fix * scale)[:, :STEPS]
    for copy in near + copies_a + copies_b:
        copy.wait_send()


def shards(state_field, adjoint, target, conductivity):
    table, trig = dft_table()
    tiles = (ROWS, 8, LANES)
    rows_first = lambda field: jnp.transpose(field[0], (1, 0, 2))
    vmem, dma = pltpu.VMEM, pltpu.SemaphoreType.DMA
    f32 = jnp.float32
    anywhere = pl.BlockSpec(memory_space=pl.ANY)
    in_vmem = pl.BlockSpec(memory_space=pltpu.VMEM)
    rs, rp, spec = pl.pallas_call(
        kernel,
        out_shape=(
            jax.ShapeDtypeStruct(tiles, f32),
            jax.ShapeDtypeStruct(tiles, f32),
            jax.ShapeDtypeStruct((4, LANES, STEPS), f32),
        ),
        in_specs=[anywhere] * 5 + [in_vmem],
        out_specs=(in_vmem,) * 3,
        scratch_shapes=[
            vmem((ROWS + 2, 8, LANES), f32),
            vmem(tiles, f32),
            vmem((ROWS + 2, 8, LANES), f32),
            vmem(tiles, f32),
            vmem(tiles, f32),
            vmem((2 * STEPS, 4 * LANES), f32),
            vmem(tiles, f32),
            vmem(tiles, f32),
            vmem((2 * ROWS, LANES), f32),
            vmem((2 * ROWS, LANES), f32),
            vmem((2 * ROWS, LANES), f32),
            vmem((2 * ROWS, LANES), f32),
            vmem((ROWS, 2, 8, LANES), f32),
            vmem((ROWS, 2, 8, LANES), f32),
            vmem((OWNERS, 2 * ROWS, LANES), f32),
            vmem((OWNERS, 2 * ROWS, LANES), f32),
            vmem((8, LANES), f32),
            dma((5,)),
            dma((4,)),
            dma((4,)),
            dma((ROWS - 1,)),
            dma((ROWS - 1,)),
            dma((OWNERS - 1,)),
            dma((OWNERS - 1,)),
        ],
        compiler_params=pltpu.CompilerParams(
            collective_id=0, has_side_effects=True, vmem_limit_bytes=24 * 1024 * 1024
        ),
    )(
        rows_first(state_field), rows_first(adjoint), rows_first(target),
        jnp.transpose(conductivity, (1, 0, 2)), jnp.asarray(table), jnp.asarray(trig),
    )
    back = lambda tile: jnp.transpose(tile, (1, 0, 2))[None]
    spectral = jnp.transpose(spec.reshape(4, 8, BLOCK, STEPS), (0, 3, 1, 2))
    return back(rs), back(rp), spectral


def solution(mesh):
    placed = (
        P("tm", "space", None, None),
        P("tm", "space", None, None),
        P("tm", "space", None, None),
        P("space", None, None),
    )
    return jax.shard_map(
        shards,
        mesh=mesh,
        in_specs=placed,
        out_specs=(
            P("tm", "space", None, None),
            P("tm", "space", None, None),
            P(None, None, "space", "tm"),
        ),
        check_vma=False,
    )
```

```python
import functools
import math

import jax
import jax.numpy as jnp
import numpy as np
from jax import lax
from jax.experimental import pallas as pl
from jax.experimental.pallas import tpu as pltpu
from jax.sharding import PartitionSpec as P

diffusion = 0.05
control_cost = 0.2
tracking = 0.5

STEPS = 96
ROWS = 12
OWNERS = 8
BLOCK = 16
TERMS = 2 * STEPS
LANES = 128


def dft_table():
    times = np.arange(STEPS)
    angles = (np.outer(times, times) % STEPS) * (2.0 * math.pi / STEPS)
    table = np.zeros((OWNERS, ROWS, 2, 4, LANES))
    for r in range(OWNERS):
        for j in range(ROWS):
            for field in range(2):
                table[r, j, field, 2 * field, :STEPS] = np.cos(angles[8 * j + r])
                table[r, j, field, 2 * field + 1, :STEPS] = -np.sin(angles[8 * j + r])
    table = table.reshape(2 * STEPS, 4 * LANES) / math.sqrt(STEPS)
    trig = np.zeros((8, LANES))
    trig[0, :STEPS] = np.cos(times * (2.0 * math.pi / STEPS))
    trig[1, :STEPS] = np.sin(times * (2.0 * math.pi / STEPS))
    rows = np.zeros((8, 4 * LANES))
    rows[:, :LANES] = trig
    return np.concatenate([table, rows]).astype(np.float32)


def swap_blocks(tile):
    row = lax.broadcasted_iota(jnp.int32, (8, LANES), 0)
    block = lax.broadcasted_iota(jnp.int32, (8, LANES), 1) // BLOCK
    for bit in (1, 2, 4):
        row_set = (row & bit) != 0
        block_set = (block & bit) != 0
        up = pltpu.roll(pltpu.roll(tile, 8 - bit, 0), BLOCK * bit, 1)
        if bit == 4:
            tile = jnp.where(row_set == block_set, tile, up)
        else:
            down = pltpu.roll(pltpu.roll(tile, bit, 0), LANES - BLOCK * bit, 1)
            tile = jnp.where(row_set == block_set, tile, jnp.where(block_set, up, down))
    return tile


def kernel(
    s_hbm, p_hbm, target_hbm, cond_hbm, table_hbm,
    rs_ref, rp_ref, recv_b, own_cond, table_v,
    s_pad, p_v, w_pad, target_v, cond_v,
    s_prev, p_next, edge_low, edge_high, from_low, from_high,
    send_a, recv_a, send_b, cond_rows,
    load_sem, near_send, near_recv, a_send, a_recv, b_send, b_recv,
):
    tm = lax.axis_index("tm")
    space = lax.axis_index("space")
    group = lax.div(tm, OWNERS)
    rank = lax.rem(tm, OWNERS)
    later = lax.rem(tm + 1, STEPS)
    earlier = lax.rem(tm + STEPS - 1, STEPS)
    above = lax.rem(space + 1, 8)
    below = lax.rem(space + 7, 8)

    loads = [
        pltpu.make_async_copy(source, target, load_sem.at[i])
        for i, (source, target) in enumerate(
            (
                (s_hbm, s_pad.at[pl.ds(1, ROWS)]),
                (p_hbm, p_v),
                (cond_hbm, cond_v),
                (target_hbm, target_v),
                (table_hbm, table_v),
            )
        )
    ]
    for load in loads:
        load.start()

    barrier = pltpu.get_barrier_semaphore()
    a_peers = [lax.rem(group + k, ROWS) for k in range(1, ROWS)]
    b_peers = [lax.rem(rank + k, OWNERS) for k in range(1, OWNERS)]
    for where in (
        [{"tm": later}, {"tm": earlier}, {"space": above}, {"space": below}]
        + [{"tm": peer * OWNERS + rank} for peer in a_peers]
        + [{"tm": group * OWNERS + peer} for peer in b_peers]
    ):
        pl.semaphore_signal(barrier, 1, device_id=where, device_id_type=pl.DeviceIdType.MESH)

    zero = jnp.zeros((8, LANES), jnp.float32)
    for padded in (s_pad, w_pad):
        padded[0] = zero
        padded[ROWS + 1] = zero
    for load in loads[:3]:
        load.wait()
    for x in range(ROWS):
        w_pad[x + 1] = cond_v[x] * p_v[x]
    for edge, z in ((edge_low, 0), (edge_high, 7)):
        edge[0:ROWS] = s_pad[1 : ROWS + 1, z, :]
        edge[ROWS : 2 * ROWS] = w_pad[1 : ROWS + 1, z, :]

    pl.semaphore_wait(barrier, 4 + ROWS - 1 + OWNERS - 1)

    def send(source, target, send_sem, recv_sem, where):
        copy = pltpu.make_async_remote_copy(
            src_ref=source, dst_ref=target, send_sem=send_sem, recv_sem=recv_sem,
            device_id=where, device_id_type=pl.DeviceIdType.MESH,
        )
        copy.start()
        return copy

    near = [
        send(s_pad.at[pl.ds(1, ROWS)], s_prev, near_send.at[0], near_recv.at[0], {"tm": later}),
        send(p_v, p_next, near_send.at[1], near_recv.at[1], {"tm": earlier}),
        send(edge_low, from_high, near_send.at[2], near_recv.at[2], {"space": below}),
        send(edge_high, from_low, near_send.at[3], near_recv.at[3], {"space": above}),
    ]

    cond_rows[...] = swap_blocks(cond_v[group])
    own_cond[...] = jnp.broadcast_to(cond_rows[pl.ds(rank, 1)], (LANES, LANES)).T

    row = lax.broadcasted_iota(jnp.int32, (8, LANES), 0)
    lane = lax.broadcasted_iota(jnp.int32, (8, LANES), 1)
    loads[3].wait()
    for copy in near:
        copy.wait_recv()

    def around(padded, x, low, high):
        centre = padded[x + 1]
        low = jnp.broadcast_to(jnp.where(space == 0, 0.0, low), (8, LANES))
        high = jnp.broadcast_to(jnp.where(space == 7, 0.0, high), (8, LANES))
        z_low = jnp.where(row == 0, low, pltpu.roll(centre, 1, 0))
        z_high = jnp.where(row == 7, high, pltpu.roll(centre, 7, 0))
        y_low = jnp.where(lane == 0, 0.0, pltpu.roll(centre, 1, 1))
        y_high = jnp.where(lane == LANES - 1, 0.0, pltpu.roll(centre, LANES - 1, 1))
        return (z_low + z_high) + (padded[x] + padded[x + 2]) + (y_low + y_high)

    for x in range(ROWS):
        s, p, w, cond = s_pad[x + 1], p_v[x], w_pad[x + 1], cond_v[x]
        around_s = around(s_pad, x, from_low[x : x + 1], from_high[x : x + 1])
        around_w = around(
            w_pad, x, from_low[ROWS + x : ROWS + x + 1], from_high[ROWS + x : ROWS + x + 1]
        )
        rs = s - s_prev[x] + diffusion * (cond * (6.0 * s - around_s)) - control_cost * p
        rp = p - p_next[x] + diffusion * (6.0 * w - around_w) + tracking * (s - target_v[x])
        rs_ref[x] = rs
        rp_ref[x] = rp
        send_a[x, 0] = swap_blocks(rs)
        send_a[x, 1] = swap_blocks(rp)

    copies_a = [
        send(send_a.at[peer], recv_a.at[group], a_send.at[k], a_recv.at[k],
             {"tm": peer * OWNERS + rank})
        for k, peer in enumerate(a_peers)
    ]
    recv_a[group] = send_a[group]
    for copy in copies_a:
        copy.wait_recv()
    for block in range(OWNERS):
        for part in range(3):
            send_b[block, 8 * part : 8 * part + 8] = recv_a[
                4 * part : 4 * part + 4, :, block, :
            ].reshape(8, LANES)
    copies_b = [
        send(send_b.at[peer], recv_b.at[rank], b_send.at[k], b_recv.at[k],
             {"tm": group * OWNERS + peer})
        for k, peer in enumerate(b_peers)
    ]
    recv_b[rank] = send_b[rank]
    loads[4].wait()
    for copy in copies_b:
        copy.wait_recv()

    for copy in near + copies_a + copies_b:
        copy.wait_send()


def solve(
    rs_ref, rp_ref, recv_b, own_cond, table_v,
    rs_hbm, rp_hbm, spec_hbm,
    spec_v, sem,
):
    copies = [
        pltpu.make_async_copy(rs_ref, rs_hbm, sem.at[0]),
        pltpu.make_async_copy(rp_ref, rp_hbm, sem.at[1]),
    ]
    for copy in copies:
        copy.start()
    spectra = lax.dot_general(
        recv_b[...].reshape(2 * STEPS, LANES), table_v[0:TERMS], (((0,), (0,)), ((), ())),
        precision=lax.Precision.HIGHEST, preferred_element_type=jnp.float32,
    )
    state_real, state_imag, adjoint_real, adjoint_imag = (
        spectra[:, LANES * i : LANES * (i + 1)] for i in range(4)
    )
    cosine, sine = table_v[TERMS : TERMS + 1, :LANES], table_v[TERMS + 1 : TERMS + 2, :LANES]
    diagonal = 1.0 + diffusion * 6.0 * own_cond[...] - cosine
    scale = 1.0 / (diagonal * diagonal + sine * sine + control_cost * tracking)
    fixes = (
        diagonal * state_real + sine * state_imag + control_cost * adjoint_real,
        diagonal * state_imag - sine * state_real + control_cost * adjoint_imag,
        diagonal * adjoint_real - sine * adjoint_imag - tracking * state_real,
        diagonal * adjoint_imag + sine * adjoint_real - tracking * state_imag,
    )
    for i, fix in enumerate(fixes):
        spec_v[i] = (fix * scale)[:, :STEPS]
        copy = pltpu.make_async_copy(spec_v.at[i], spec_hbm.at[i], sem.at[2 + i])
        copy.start()
        copies.append(copy)
    for copy in copies:
        copy.wait()


def shards(state_field, adjoint, target, conductivity):
    table = dft_table()
    tiles = (ROWS, 8, LANES)
    stay = lambda array: pltpu.with_memory_space_constraint(array, pltpu.HBM)
    rows_first = lambda field: stay(jnp.transpose(field[0], (1, 0, 2)))
    vmem, dma = pltpu.VMEM, pltpu.SemaphoreType.DMA
    f32 = jnp.float32
    in_hbm = pl.BlockSpec(memory_space=pltpu.HBM)
    in_vmem = pl.BlockSpec(memory_space=pltpu.VMEM)
    rs, rp, got, own_cond, table = pl.pallas_call(
        kernel,
        out_shape=(
            jax.ShapeDtypeStruct(tiles, f32),
            jax.ShapeDtypeStruct(tiles, f32),
            jax.ShapeDtypeStruct((OWNERS, 2 * ROWS, LANES), f32),
            jax.ShapeDtypeStruct((LANES, LANES), f32),
            jax.ShapeDtypeStruct((TERMS + 8, 4 * LANES), f32),
        ),
        in_specs=[in_hbm] * 5,
        out_specs=(in_vmem,) * 5,
        scratch_shapes=[
            vmem((ROWS + 2, 8, LANES), f32),
            vmem(tiles, f32),
            vmem((ROWS + 2, 8, LANES), f32),
            vmem(tiles, f32),
            vmem(tiles, f32),
            vmem(tiles, f32),
            vmem(tiles, f32),
            vmem((2 * ROWS, LANES), f32),
            vmem((2 * ROWS, LANES), f32),
            vmem((2 * ROWS, LANES), f32),
            vmem((2 * ROWS, LANES), f32),
            vmem((ROWS, 2, 8, LANES), f32),
            vmem((ROWS, 2, 8, LANES), f32),
            vmem((OWNERS, 2 * ROWS, LANES), f32),
            vmem((8, LANES), f32),
            dma((5,)),
            dma((4,)),
            dma((4,)),
            dma((ROWS - 1,)),
            dma((ROWS - 1,)),
            dma((OWNERS - 1,)),
            dma((OWNERS - 1,)),
        ],
        compiler_params=pltpu.CompilerParams(
            collective_id=0, has_side_effects=True, vmem_limit_bytes=24 * 1024 * 1024
        ),
    )(
        rows_first(state_field), rows_first(adjoint), rows_first(target),
        stay(jnp.transpose(conductivity, (1, 0, 2))), stay(jnp.asarray(table)),
    )
    rs, rp, spec = pl.pallas_call(
        solve,
        out_shape=(
            jax.ShapeDtypeStruct(tiles, f32),
            jax.ShapeDtypeStruct(tiles, f32),
            jax.ShapeDtypeStruct((4, LANES, STEPS), f32),
        ),
        in_specs=[in_vmem] * 5,
        out_specs=(in_hbm,) * 3,
        scratch_shapes=[vmem((4, LANES, STEPS), f32), dma((6,))],
        compiler_params=pltpu.CompilerParams(vmem_limit_bytes=16 * 1024 * 1024),
    )(rs, rp, got, own_cond, table)
    back = lambda tile: jnp.transpose(tile, (1, 0, 2))[None]
    spectral = jnp.transpose(spec.reshape(4, 8, BLOCK, STEPS), (0, 3, 1, 2))
    return back(rs), back(rp), spectral


def solution(mesh):
    placed = (
        P("tm", "space", None, None),
        P("tm", "space", None, None),
        P("tm", "space", None, None),
        P("space", None, None),
    )
    return jax.shard_map(
        shards,
        mesh=mesh,
        in_specs=placed,
        out_specs=(
            P("tm", "space", None, None),
            P("tm", "space", None, None),
            P(None, None, "space", "tm"),
        ),
        check_vma=False,
    )
```

```python
import functools
import math

import jax
import jax.numpy as jnp
import numpy as np
from jax import lax
from jax.experimental import pallas as pl
from jax.experimental.pallas import tpu as pltpu
from jax.sharding import PartitionSpec as P

diffusion = 0.05
control_cost = 0.2
tracking = 0.5

STEPS = 96
DEPTH = 12
ROWS = 12
OWNERS = 8
BLOCK = 16
TERMS = 2 * STEPS
LANES = 128


def dft_table():
    times = np.arange(STEPS)
    angles = (np.outer(times, times) % STEPS) * (2.0 * math.pi / STEPS)
    table = np.zeros((STEPS, 2, 4, LANES))
    for field in range(2):
        table[:, field, 2 * field, :STEPS] = np.cos(angles)
        table[:, field, 2 * field + 1, :STEPS] = -np.sin(angles)
    table = table.reshape(2 * STEPS, 4 * LANES) / math.sqrt(STEPS)
    trig = np.zeros((8, LANES))
    trig[0, :STEPS] = np.cos(times * (2.0 * math.pi / STEPS))
    trig[1, :STEPS] = np.sin(times * (2.0 * math.pi / STEPS))
    rows = np.zeros((8, 4 * LANES))
    rows[:, :LANES] = trig
    return np.concatenate([table, rows]).astype(np.float32)


def swap_blocks(tile):
    row = lax.broadcasted_iota(jnp.int32, (8, LANES), 0)
    block = lax.broadcasted_iota(jnp.int32, (8, LANES), 1) // BLOCK
    for bit in (1, 2, 4):
        row_set = (row & bit) != 0
        block_set = (block & bit) != 0
        up = pltpu.roll(pltpu.roll(tile, 8 - bit, 0), BLOCK * bit, 1)
        if bit == 4:
            tile = jnp.where(row_set == block_set, tile, up)
        else:
            down = pltpu.roll(pltpu.roll(tile, bit, 0), LANES - BLOCK * bit, 1)
            tile = jnp.where(row_set == block_set, tile, jnp.where(block_set, up, down))
    return tile


def kernel(
    s_hbm, p_hbm, target_hbm, cond_hbm, table_hbm,
    rs_ref, rp_ref, got, own_cond, table_v,
    s_pad, p_v, w_pad, target_v, cond_v,
    s_prev, p_next, edge_low, edge_high, from_low, from_high,
    blocks, cond_rows,
    load_sem, near_send, near_recv, block_send, block_recv,
):
    tm = lax.axis_index("tm")
    space = lax.axis_index("space")
    group = lax.div(tm, OWNERS)
    rank = lax.rem(tm, OWNERS)
    later = lax.rem(tm + 1, STEPS)
    earlier = lax.rem(tm + STEPS - 1, STEPS)
    above = lax.rem(space + 1, 8)
    below = lax.rem(space + 7, 8)

    loads = [
        pltpu.make_async_copy(source, target, load_sem.at[i])
        for i, (source, target) in enumerate(
            (
                (s_hbm, s_pad.at[pl.ds(1, ROWS)]),
                (p_hbm, p_v),
                (cond_hbm, cond_v),
                (target_hbm, target_v),
                (table_hbm, table_v),
            )
        )
    ]
    for load in loads:
        load.start()

    barrier = pltpu.get_barrier_semaphore()
    for where in ({"space": above}, {"space": below}):
        pl.semaphore_signal(barrier, 1, device_id=where, device_id_type=pl.DeviceIdType.MESH)

    x, y, z = lax.div(tm, 2 * DEPTH), lax.rem(tm, 2), lax.rem(lax.div(tm, 2), DEPTH)

    def partner(i):
        level = lax.div(i, 8)
        away = 6 - lax.div(level + 1, 2)
        away = away + lax.rem(level, 2) * (DEPTH - 2 * away)
        to_x = lax.rem(x + lax.div(lax.rem(i, 8), 2) + 1, 4)
        to_y = lax.rem(y + i + 1, 2)
        return 2 * DEPTH * to_x + 2 * lax.rem(z + away, DEPTH) + to_y

    def greet(i, carry):
        pl.semaphore_signal(
            barrier, 1, device_id={"tm": partner(i)}, device_id_type=pl.DeviceIdType.MESH
        )
        return carry

    lax.fori_loop(0, STEPS - 1, greet, 0)

    zero = jnp.zeros((8, LANES), jnp.float32)
    for padded in (s_pad, w_pad):
        padded[0] = zero
        padded[ROWS + 1] = zero
    for load in loads[:3]:
        load.wait()
    for i in range(ROWS):
        w_pad[i + 1] = cond_v[i] * p_v[i]
    for edge, plane in ((edge_low, 0), (edge_high, 7)):
        edge[0:ROWS] = s_pad[1 : ROWS + 1, plane, :]
        edge[ROWS : 2 * ROWS] = w_pad[1 : ROWS + 1, plane, :]

    pl.semaphore_wait(barrier, STEPS - 1 + 2)

    def send(source, target, send_sem, recv_sem, where):
        copy = pltpu.make_async_remote_copy(
            src_ref=source, dst_ref=target, send_sem=send_sem, recv_sem=recv_sem,
            device_id=where, device_id_type=pl.DeviceIdType.MESH,
        )
        copy.start()
        return copy

    near = [
        send(s_pad.at[pl.ds(1, ROWS)], s_prev, near_send.at[0], near_recv.at[0], {"tm": later}),
        send(p_v, p_next, near_send.at[1], near_recv.at[1], {"tm": earlier}),
        send(edge_low, from_high, near_send.at[2], near_recv.at[2], {"space": below}),
        send(edge_high, from_low, near_send.at[3], near_recv.at[3], {"space": above}),
    ]

    cond_rows[...] = swap_blocks(cond_v[group])
    own_cond[...] = jnp.broadcast_to(cond_rows[pl.ds(rank, 1)], (LANES, LANES)).T

    row = lax.broadcasted_iota(jnp.int32, (8, LANES), 0)
    lane = lax.broadcasted_iota(jnp.int32, (8, LANES), 1)
    loads[3].wait()
    for copy in near:
        copy.wait_recv()

    def around(padded, i, low, high):
        centre = padded[i + 1]
        low = jnp.broadcast_to(jnp.where(space == 0, 0.0, low), (8, LANES))
        high = jnp.broadcast_to(jnp.where(space == 7, 0.0, high), (8, LANES))
        z_low = jnp.where(row == 0, low, pltpu.roll(centre, 1, 0))
        z_high = jnp.where(row == 7, high, pltpu.roll(centre, 7, 0))
        y_low = jnp.where(lane == 0, 0.0, pltpu.roll(centre, 1, 1))
        y_high = jnp.where(lane == LANES - 1, 0.0, pltpu.roll(centre, LANES - 1, 1))
        return (z_low + z_high) + (padded[i] + padded[i + 2]) + (y_low + y_high)

    for i in range(ROWS):
        s, p, w, cond = s_pad[i + 1], p_v[i], w_pad[i + 1], cond_v[i]
        around_s = around(s_pad, i, from_low[i : i + 1], from_high[i : i + 1])
        around_w = around(
            w_pad, i, from_low[ROWS + i : ROWS + i + 1], from_high[ROWS + i : ROWS + i + 1]
        )
        rs = s - s_prev[i] + diffusion * (cond * (6.0 * s - around_s)) - control_cost * p
        rp = p - p_next[i] + diffusion * (6.0 * w - around_w) + tracking * (s - target_v[i])
        rs_ref[i] = rs
        rp_ref[i] = rp
        blocks[pl.ds(16 * i, 8, stride=2)] = swap_blocks(rs)
        blocks[pl.ds(16 * i + 1, 8, stride=2)] = swap_blocks(rp)

    mine = pl.ds(pl.multiple_of(2 * tm, 2), 2)
    own = pltpu.make_async_copy(blocks.at[mine], got.at[mine], block_recv)
    own.start()

    def hand_out(i, carry):
        peer = partner(i)
        theirs = pl.ds(pl.multiple_of(2 * peer, 2), 2)
        send(blocks.at[theirs], got.at[mine], block_send, block_recv, {"tm": peer})
        return carry

    lax.fori_loop(0, STEPS - 1, hand_out, 0)
    loads[4].wait()
    pltpu.make_async_copy(got, got, block_recv).wait()
    sent = blocks.at[pl.ds(0, TERMS - 2)]
    pltpu.make_async_copy(sent, sent, block_send).wait()
    for copy in near:
        copy.wait_send()


def solve(
    rs_ref, rp_ref, got, own_cond, table_v,
    rs_hbm, rp_hbm, spec_hbm,
    spec_v, sem,
):
    copies = [
        pltpu.make_async_copy(rs_ref, rs_hbm, sem.at[0]),
        pltpu.make_async_copy(rp_ref, rp_hbm, sem.at[1]),
    ]
    for copy in copies:
        copy.start()
    spectra = lax.dot_general(
        got[...], table_v[0:TERMS], (((0,), (0,)), ((), ())),
        precision=lax.Precision.HIGHEST, preferred_element_type=jnp.float32,
    )
    state_real, state_imag, adjoint_real, adjoint_imag = (
        spectra[:, LANES * i : LANES * (i + 1)] for i in range(4)
    )
    cosine, sine = table_v[TERMS : TERMS + 1, :LANES], table_v[TERMS + 1 : TERMS + 2, :LANES]
    diagonal = 1.0 + diffusion * 6.0 * own_cond[...] - cosine
    scale = 1.0 / (diagonal * diagonal + sine * sine + control_cost * tracking)
    fixes = (
        diagonal * state_real + sine * state_imag + control_cost * adjoint_real,
        diagonal * state_imag - sine * state_real + control_cost * adjoint_imag,
        diagonal * adjoint_real - sine * adjoint_imag - tracking * state_real,
        diagonal * adjoint_imag + sine * adjoint_real - tracking * state_imag,
    )
    for i, fix in enumerate(fixes):
        spec_v[i] = (fix * scale)[:, :STEPS]
        copy = pltpu.make_async_copy(spec_v.at[i], spec_hbm.at[i], sem.at[2 + i])
        copy.start()
        copies.append(copy)
    for copy in copies:
        copy.wait()


def shards(state_field, adjoint, target, conductivity):
    table = dft_table()
    tiles = (ROWS, 8, LANES)
    stay = lambda array: pltpu.with_memory_space_constraint(array, pltpu.HBM)
    rows_first = lambda field: stay(jnp.transpose(field[0], (1, 0, 2)))
    vmem, dma = pltpu.VMEM, pltpu.SemaphoreType.DMA
    f32 = jnp.float32
    in_hbm = pl.BlockSpec(memory_space=pltpu.HBM)
    in_vmem = pl.BlockSpec(memory_space=pltpu.VMEM)
    rs, rp, got, own_cond, table = pl.pallas_call(
        kernel,
        out_shape=(
            jax.ShapeDtypeStruct(tiles, f32),
            jax.ShapeDtypeStruct(tiles, f32),
            jax.ShapeDtypeStruct((TERMS, LANES), f32),
            jax.ShapeDtypeStruct((LANES, LANES), f32),
            jax.ShapeDtypeStruct((TERMS + 8, 4 * LANES), f32),
        ),
        in_specs=[in_hbm] * 5,
        out_specs=(in_vmem,) * 5,
        scratch_shapes=[
            vmem((ROWS + 2, 8, LANES), f32),
            vmem(tiles, f32),
            vmem((ROWS + 2, 8, LANES), f32),
            vmem(tiles, f32),
            vmem(tiles, f32),
            vmem(tiles, f32),
            vmem(tiles, f32),
            vmem((2 * ROWS, LANES), f32),
            vmem((2 * ROWS, LANES), f32),
            vmem((2 * ROWS, LANES), f32),
            vmem((2 * ROWS, LANES), f32),
            vmem((TERMS, LANES), f32),
            vmem((8, LANES), f32),
            dma((5,)),
            dma((4,)),
            dma((4,)),
            dma,
            dma,
        ],
        compiler_params=pltpu.CompilerParams(
            collective_id=0, has_side_effects=True, vmem_limit_bytes=24 * 1024 * 1024
        ),
    )(
        rows_first(state_field), rows_first(adjoint), rows_first(target),
        stay(jnp.transpose(conductivity, (1, 0, 2))), stay(jnp.asarray(table)),
    )
    rs, rp, spec = pl.pallas_call(
        solve,
        out_shape=(
            jax.ShapeDtypeStruct(tiles, f32),
            jax.ShapeDtypeStruct(tiles, f32),
            jax.ShapeDtypeStruct((4, LANES, STEPS), f32),
        ),
        in_specs=[in_vmem] * 5,
        out_specs=(in_hbm,) * 3,
        scratch_shapes=[vmem((4, LANES, STEPS), f32), dma((6,))],
        compiler_params=pltpu.CompilerParams(vmem_limit_bytes=16 * 1024 * 1024),
    )(rs, rp, got, own_cond, table)
    back = lambda tile: jnp.transpose(tile, (1, 0, 2))[None]
    spectral = jnp.transpose(spec.reshape(4, 8, BLOCK, STEPS), (0, 3, 1, 2))
    return back(rs), back(rp), spectral


def solution(mesh):
    placed = (
        P("tm", "space", None, None),
        P("tm", "space", None, None),
        P("tm", "space", None, None),
        P("space", None, None),
    )
    return jax.shard_map(
        shards,
        mesh=mesh,
        in_specs=placed,
        out_specs=(
            P("tm", "space", None, None),
            P("tm", "space", None, None),
            P(None, None, "space", "tm"),
        ),
        check_vma=False,
    )
```

```python
import functools
import math

import jax
import jax.numpy as jnp
import numpy as np
from jax import lax
from jax.experimental import pallas as pl
from jax.experimental.pallas import tpu as pltpu
from jax.sharding import PartitionSpec as P

diffusion = 0.05
control_cost = 0.2
tracking = 0.5

STEPS = 96
DEPTH = 12
ROWS = 12
OWNERS = 8
BLOCK = 16
TERMS = 2 * STEPS
LANES = 128


def dft_table():
    times = np.arange(STEPS)
    angles = (np.outer(times, times) % STEPS) * (2.0 * math.pi / STEPS)
    table = np.zeros((STEPS, 2, 4, LANES))
    for field in range(2):
        table[:, field, 2 * field, :STEPS] = np.cos(angles)
        table[:, field, 2 * field + 1, :STEPS] = -np.sin(angles)
    table = table.reshape(2 * STEPS, 4 * LANES) / math.sqrt(STEPS)
    trig = np.zeros((8, LANES))
    trig[0, :STEPS] = np.cos(times * (2.0 * math.pi / STEPS))
    trig[1, :STEPS] = np.sin(times * (2.0 * math.pi / STEPS))
    rows = np.zeros((8, 4 * LANES))
    rows[:, :LANES] = trig
    return np.concatenate([table, rows]).astype(np.float32)


def swap_blocks(tile):
    row = lax.broadcasted_iota(jnp.int32, (8, LANES), 0)
    block = lax.broadcasted_iota(jnp.int32, (8, LANES), 1) // BLOCK
    for bit in (1, 2, 4):
        row_set = (row & bit) != 0
        block_set = (block & bit) != 0
        up = pltpu.roll(pltpu.roll(tile, 8 - bit, 0), BLOCK * bit, 1)
        if bit == 4:
            tile = jnp.where(row_set == block_set, tile, up)
        else:
            down = pltpu.roll(pltpu.roll(tile, bit, 0), LANES - BLOCK * bit, 1)
            tile = jnp.where(row_set == block_set, tile, jnp.where(block_set, up, down))
    return tile


def kernel(
    s_hbm, p_hbm, target_hbm, cond_hbm, table_hbm,
    rs_ref, rp_ref, got, own_cond, table_v,
    s_pad, p_v, w_pad, target_v, cond_v,
    s_prev, p_next, edge_low, edge_high, from_low, from_high,
    blocks, cond_rows,
    load_sem, near_send, near_recv, block_send, block_recv, token, ready,
):
    tm = lax.axis_index("tm")
    space = lax.axis_index("space")
    group = lax.div(tm, OWNERS)
    rank = lax.rem(tm, OWNERS)
    later = lax.rem(tm + 1, STEPS)
    earlier = lax.rem(tm + STEPS - 1, STEPS)
    above = lax.rem(space + 1, 8)
    below = lax.rem(space + 7, 8)

    loads = [
        pltpu.make_async_copy(source, target, load_sem.at[i])
        for i, (source, target) in enumerate(
            (
                (s_hbm, s_pad.at[pl.ds(1, ROWS)]),
                (p_hbm, p_v),
                (cond_hbm, cond_v),
                (target_hbm, target_v),
                (table_hbm, table_v),
            )
        )
    ]
    for load in loads:
        load.start()

    x, y, z = lax.div(tm, 2 * DEPTH), lax.rem(tm, 2), lax.rem(lax.div(tm, 2), DEPTH)

    def at_plane(plane, j):
        return 2 * DEPTH * lax.rem(x + j // 2, 4) + 2 * plane + lax.rem(y + j, 2)

    def signal(semaphore, where):
        pl.semaphore_signal(semaphore, 1, device_id=where, device_id_type=pl.DeviceIdType.MESH)

    barrier = pltpu.get_barrier_semaphore()
    signal(barrier, {"space": above})
    signal(barrier, {"space": below})
    signal(barrier, {"tm": lax.rem(tm + STEPS - 1 + 2 * y, STEPS)})

    @pl.when(z > 0)
    def _():
        signal(barrier, {"tm": tm - 2})

    @pl.when(z < DEPTH - 1)
    def _():
        signal(barrier, {"tm": tm + 2})

    for j in range(1, 8):
        signal(barrier, {"tm": at_plane(z, j)})

    zero = jnp.zeros((8, LANES), jnp.float32)
    for padded in (s_pad, w_pad):
        padded[0] = zero
        padded[ROWS + 1] = zero
    for load in loads[:3]:
        load.wait()
    for i in range(ROWS):
        w_pad[i + 1] = cond_v[i] * p_v[i]
    for edge, plane in ((edge_low, 0), (edge_high, 7)):
        edge[0:ROWS] = s_pad[1 : ROWS + 1, plane, :]
        edge[ROWS : 2 * ROWS] = w_pad[1 : ROWS + 1, plane, :]

    pl.semaphore_wait(barrier, 10 + (z + 10) // (DEPTH - 1) + (21 - z) // (DEPTH - 1))

    def send(source, target, send_sem, recv_sem, where):
        copy = pltpu.make_async_remote_copy(
            src_ref=source, dst_ref=target, send_sem=send_sem, recv_sem=recv_sem,
            device_id=where, device_id_type=pl.DeviceIdType.MESH,
        )
        copy.start()
        return copy

    near = [
        send(s_pad.at[pl.ds(1, ROWS)], s_prev, near_send.at[0], near_recv.at[0], {"tm": later}),
        send(p_v, p_next, near_send.at[1], near_recv.at[1], {"tm": earlier}),
        send(edge_low, from_high, near_send.at[2], near_recv.at[2], {"space": below}),
        send(edge_high, from_low, near_send.at[3], near_recv.at[3], {"space": above}),
    ]

    @pl.when(z > 0)
    def _():
        pl.semaphore_wait(token, 1)

    @pl.when(z < DEPTH - 1)
    def _():
        @pl.when(y == 1)
        def _():
            signal(token, {"tm": tm + 2})
            signal(token, {"tm": tm + 1})

    def announce(plane, carry):
        signal(ready, {"tm": at_plane(plane, 0)})
        return carry

    lax.fori_loop(0, z, announce, 0)

    cond_rows[...] = swap_blocks(cond_v[group])
    own_cond[...] = jnp.broadcast_to(cond_rows[pl.ds(rank, 1)], (LANES, LANES)).T

    row = lax.broadcasted_iota(jnp.int32, (8, LANES), 0)
    lane = lax.broadcasted_iota(jnp.int32, (8, LANES), 1)
    loads[3].wait()
    for copy in near:
        copy.wait_recv()

    def around(padded, i, low, high):
        centre = padded[i + 1]
        low = jnp.broadcast_to(jnp.where(space == 0, 0.0, low), (8, LANES))
        high = jnp.broadcast_to(jnp.where(space == 7, 0.0, high), (8, LANES))
        z_low = jnp.where(row == 0, low, pltpu.roll(centre, 1, 0))
        z_high = jnp.where(row == 7, high, pltpu.roll(centre, 7, 0))
        y_low = jnp.where(lane == 0, 0.0, pltpu.roll(centre, 1, 1))
        y_high = jnp.where(lane == LANES - 1, 0.0, pltpu.roll(centre, LANES - 1, 1))
        return (z_low + z_high) + (padded[i] + padded[i + 2]) + (y_low + y_high)

    for i in range(ROWS):
        s, p, w, cond = s_pad[i + 1], p_v[i], w_pad[i + 1], cond_v[i]
        around_s = around(s_pad, i, from_low[i : i + 1], from_high[i : i + 1])
        around_w = around(
            w_pad, i, from_low[ROWS + i : ROWS + i + 1], from_high[ROWS + i : ROWS + i + 1]
        )
        rs = s - s_prev[i] + diffusion * (cond * (6.0 * s - around_s)) - control_cost * p
        rp = p - p_next[i] + diffusion * (6.0 * w - around_w) + tracking * (s - target_v[i])
        rs_ref[i] = rs
        rp_ref[i] = rp
        blocks[pl.ds(16 * i, 8, stride=2)] = swap_blocks(rs)
        blocks[pl.ds(16 * i + 1, 8, stride=2)] = swap_blocks(rp)

    mine = pl.ds(pl.multiple_of(2 * tm, 2), 2)
    own = pltpu.make_async_copy(blocks.at[mine], got.at[mine], block_recv)
    own.start()

    def serve(plane, first):
        for j in range(first, 8):
            peer = at_plane(plane, j)
            theirs = pl.ds(pl.multiple_of(2 * peer, 2), 2)
            send(blocks.at[theirs], got.at[mine], block_send, block_recv, {"tm": peer})

    def serve_plane(plane, carry):
        serve(plane, 0)
        return carry

    lax.fori_loop(0, z, serve_plane, 0)
    serve(z, 1)

    @pl.when(z < DEPTH - 1)
    def _():
        pl.semaphore_wait(ready, DEPTH - 1 - z)

    lax.fori_loop(z + 1, DEPTH, serve_plane, 0)
    loads[4].wait()
    pltpu.make_async_copy(got, got, block_recv).wait()
    sent = blocks.at[pl.ds(0, TERMS - 2)]
    pltpu.make_async_copy(sent, sent, block_send).wait()
    for copy in near:
        copy.wait_send()


def solve(
    rs_ref, rp_ref, got, own_cond, table_v,
    rs_hbm, rp_hbm, spec_hbm,
    spec_v, sem,
):
    copies = [
        pltpu.make_async_copy(rs_ref, rs_hbm, sem.at[0]),
        pltpu.make_async_copy(rp_ref, rp_hbm, sem.at[1]),
    ]
    for copy in copies:
        copy.start()
    spectra = lax.dot_general(
        got[...], table_v[0:TERMS], (((0,), (0,)), ((), ())),
        precision=lax.Precision.HIGHEST, preferred_element_type=jnp.float32,
    )
    state_real, state_imag, adjoint_real, adjoint_imag = (
        spectra[:, LANES * i : LANES * (i + 1)] for i in range(4)
    )
    cosine, sine = table_v[TERMS : TERMS + 1, :LANES], table_v[TERMS + 1 : TERMS + 2, :LANES]
    diagonal = 1.0 + diffusion * 6.0 * own_cond[...] - cosine
    scale = 1.0 / (diagonal * diagonal + sine * sine + control_cost * tracking)
    fixes = (
        diagonal * state_real + sine * state_imag + control_cost * adjoint_real,
        diagonal * state_imag - sine * state_real + control_cost * adjoint_imag,
        diagonal * adjoint_real - sine * adjoint_imag - tracking * state_real,
        diagonal * adjoint_imag + sine * adjoint_real - tracking * state_imag,
    )
    for i, fix in enumerate(fixes):
        spec_v[i] = (fix * scale)[:, :STEPS]
        copy = pltpu.make_async_copy(spec_v.at[i], spec_hbm.at[i], sem.at[2 + i])
        copy.start()
        copies.append(copy)
    for copy in copies:
        copy.wait()


def shards(state_field, adjoint, target, conductivity):
    table = dft_table()
    tiles = (ROWS, 8, LANES)
    stay = lambda array: pltpu.with_memory_space_constraint(array, pltpu.HBM)
    rows_first = lambda field: stay(jnp.transpose(field[0], (1, 0, 2)))
    vmem, dma = pltpu.VMEM, pltpu.SemaphoreType.DMA
    f32 = jnp.float32
    in_hbm = pl.BlockSpec(memory_space=pltpu.HBM)
    in_vmem = pl.BlockSpec(memory_space=pltpu.VMEM)
    rs, rp, got, own_cond, table = pl.pallas_call(
        kernel,
        out_shape=(
            jax.ShapeDtypeStruct(tiles, f32),
            jax.ShapeDtypeStruct(tiles, f32),
            jax.ShapeDtypeStruct((TERMS, LANES), f32),
            jax.ShapeDtypeStruct((LANES, LANES), f32),
            jax.ShapeDtypeStruct((TERMS + 8, 4 * LANES), f32),
        ),
        in_specs=[in_hbm] * 5,
        out_specs=(in_vmem,) * 5,
        scratch_shapes=[
            vmem((ROWS + 2, 8, LANES), f32),
            vmem(tiles, f32),
            vmem((ROWS + 2, 8, LANES), f32),
            vmem(tiles, f32),
            vmem(tiles, f32),
            vmem(tiles, f32),
            vmem(tiles, f32),
            vmem((2 * ROWS, LANES), f32),
            vmem((2 * ROWS, LANES), f32),
            vmem((2 * ROWS, LANES), f32),
            vmem((2 * ROWS, LANES), f32),
            vmem((TERMS, LANES), f32),
            vmem((8, LANES), f32),
            dma((5,)),
            dma((4,)),
            dma((4,)),
            dma,
            dma,
            pltpu.SemaphoreType.REGULAR,
            pltpu.SemaphoreType.REGULAR,
        ],
        compiler_params=pltpu.CompilerParams(
            collective_id=0, has_side_effects=True, vmem_limit_bytes=24 * 1024 * 1024
        ),
    )(
        rows_first(state_field), rows_first(adjoint), rows_first(target),
        stay(jnp.transpose(conductivity, (1, 0, 2))), stay(jnp.asarray(table)),
    )
    rs, rp, spec = pl.pallas_call(
        solve,
        out_shape=(
            jax.ShapeDtypeStruct(tiles, f32),
            jax.ShapeDtypeStruct(tiles, f32),
            jax.ShapeDtypeStruct((4, LANES, STEPS), f32),
        ),
        in_specs=[in_vmem] * 5,
        out_specs=(in_hbm,) * 3,
        scratch_shapes=[vmem((4, LANES, STEPS), f32), dma((6,))],
        compiler_params=pltpu.CompilerParams(vmem_limit_bytes=16 * 1024 * 1024),
    )(rs, rp, got, own_cond, table)
    back = lambda tile: jnp.transpose(tile, (1, 0, 2))[None]
    spectral = jnp.transpose(spec.reshape(4, 8, BLOCK, STEPS), (0, 3, 1, 2))
    return back(rs), back(rp), spectral


def solution(mesh):
    placed = (
        P("tm", "space", None, None),
        P("tm", "space", None, None),
        P("tm", "space", None, None),
        P("space", None, None),
    )
    return jax.shard_map(
        shards,
        mesh=mesh,
        in_specs=placed,
        out_specs=(
            P("tm", "space", None, None),
            P("tm", "space", None, None),
            P(None, None, "space", "tm"),
        ),
        check_vma=False,
    )
```

```python
import functools
import math

import jax
import jax.numpy as jnp
import numpy as np
from jax import lax
from jax.experimental import pallas as pl
from jax.experimental.pallas import tpu as pltpu
from jax.sharding import PartitionSpec as P

diffusion = 0.05
control_cost = 0.2
tracking = 0.5

STEPS = 96
DEPTH = 12
HALF = 8
ROWS = 12
OWNERS = 8
BLOCK = 16
TERMS = 2 * STEPS
LANES = 128


def dft_table():
    times = np.arange(STEPS)
    angles = (np.outer(times, times) % STEPS) * (2.0 * math.pi / STEPS)
    table = np.zeros((STEPS, 2, 4, LANES))
    for field in range(2):
        table[:, field, 2 * field, :STEPS] = np.cos(angles)
        table[:, field, 2 * field + 1, :STEPS] = -np.sin(angles)
    table = table.reshape(2 * STEPS, 4 * LANES) / math.sqrt(STEPS)
    trig = np.zeros((8, LANES))
    trig[0, :STEPS] = np.cos(times * (2.0 * math.pi / STEPS))
    trig[1, :STEPS] = np.sin(times * (2.0 * math.pi / STEPS))
    table = table.astype(np.float32)
    high = table.astype(jnp.bfloat16)
    return high, (table - high.astype(np.float32)).astype(jnp.bfloat16), trig.astype(np.float32)


def swap_blocks(tile):
    row = lax.broadcasted_iota(jnp.int32, (8, LANES), 0)
    block = lax.broadcasted_iota(jnp.int32, (8, LANES), 1) // BLOCK
    for bit in (1, 2, 4):
        row_set = (row & bit) != 0
        block_set = (block & bit) != 0
        up = pltpu.roll(pltpu.roll(tile, 8 - bit, 0), BLOCK * bit, 1)
        if bit == 4:
            tile = jnp.where(row_set == block_set, tile, up)
        else:
            down = pltpu.roll(pltpu.roll(tile, bit, 0), LANES - BLOCK * bit, 1)
            tile = jnp.where(row_set == block_set, tile, jnp.where(block_set, up, down))
    return tile


def kernel(
    s_hbm, p_hbm, target_hbm, cond_hbm, high_hbm, low_hbm, trig_hbm,
    rs_ref, rp_ref, got, own_cond, high_v, low_v, trig_v,
    s_v, p_v, w_v, target_v, cond_v,
    s_prev, p_next, edge_low, edge_high, from_low, from_high,
    blocks, cond_rows,
    load_sem, near_send, near_recv, block_send, block_recv, token, token_0, ready,
):
    tm = lax.axis_index("tm")
    space = lax.axis_index("space")
    group = lax.div(tm, OWNERS)
    rank = lax.rem(tm, OWNERS)
    later = lax.rem(tm + 1, STEPS)
    earlier = lax.rem(tm + STEPS - 1, STEPS)
    above = lax.rem(space + 1, 8)
    below = lax.rem(space + 7, 8)

    loads = [
        pltpu.make_async_copy(source, target, load_sem.at[i])
        for i, (source, target) in enumerate(
            (
                (s_hbm, s_v),
                (p_hbm, p_v),
                (cond_hbm, cond_v),
                (target_hbm, target_v),
                (high_hbm, high_v),
                (low_hbm, low_v),
                (trig_hbm, trig_v),
            )
        )
    ]
    x, y, z = lax.div(tm, 2 * DEPTH), lax.rem(tm, 2), lax.rem(lax.div(tm, 2), DEPTH)

    def at_plane(plane, j):
        return 2 * DEPTH * lax.rem(x + j // 2, 4) + 2 * plane + lax.rem(y + j, 2)

    def signal(semaphore, where):
        pl.semaphore_signal(semaphore, 1, device_id=where, device_id_type=pl.DeviceIdType.MESH)

    barrier = pltpu.get_barrier_semaphore()
    signal(barrier, {"space": above})
    signal(barrier, {"space": below})
    signal(barrier, {"tm": lax.rem(tm + STEPS - 1 + 2 * y, STEPS)})
    for load in loads[:3]:
        load.start()

    @pl.when(z > 0)
    def _():
        signal(barrier, {"tm": tm - 2})

    @pl.when(z < DEPTH - 1)
    def _():
        signal(barrier, {"tm": tm + 2})

    for j in range(1, 8):
        signal(barrier, {"tm": at_plane(z, j)})

    @pl.when((z >= HALF) & (space == 0))
    def _():
        signal(barrier, {"tm": 2 * DEPTH * x})

    @pl.when((z == 0) & (y == 0) & (space == 0))
    def _():
        for far in range(2 * HALF, 2 * DEPTH):
            signal(barrier, {"tm": tm + far})

    for load in loads[3:]:
        load.start()

    for load in loads[:3]:
        load.wait()
    for i in range(ROWS):
        w_v[i // 3, i % 3] = cond_v[i] * p_v[i // 3, i % 3]
    for edge, plane in ((edge_low, 0), (edge_high, 7)):
        for i in range(ROWS):
            edge[i : i + 1] = s_v[i // 3, i % 3, plane : plane + 1]
            edge[ROWS + i : ROWS + i + 1] = w_v[i // 3, i % 3, plane : plane + 1]

    last = DEPTH - 1
    greetings = 10 + (z + last - 1) // last + (2 * last - 1 - z) // last
    wrapped = (z + last - HALF) // last + 2 * (DEPTH - HALF) * (1 - y) * ((last - z) // last)
    greetings += wrapped * (1 - (space + 7) // 8)
    pl.semaphore_wait(barrier, greetings)

    def send(source, target, send_sem, recv_sem, where):
        copy = pltpu.make_async_remote_copy(
            src_ref=source, dst_ref=target, send_sem=send_sem, recv_sem=recv_sem,
            device_id=where, device_id_type=pl.DeviceIdType.MESH,
        )
        copy.start()
        return copy

    near = [
        send(edge_low, from_high, near_send.at[0], near_recv.at[0], {"space": below}),
        send(edge_high, from_low, near_send.at[1], near_recv.at[1], {"space": above}),
    ]
    for q in range(3):
        part, k = (slice(None), q), 2 + 2 * q
        near += [
            send(s_v.at[part], s_prev.at[part], near_send.at[k], near_recv.at[k], {"tm": later}),
            send(p_v.at[part], p_next.at[part], near_send.at[k + 1], near_recv.at[k + 1],
                 {"tm": earlier}),
        ]

    @pl.when(z > 1)
    def _():
        pl.semaphore_wait(token, 1)

    def hand_up(semaphore):
        signal(semaphore, {"tm": tm + 2})
        signal(semaphore, {"tm": tm + 1})

    @pl.when((y == 1) & (z > 0) & (z < DEPTH - 1))
    def _():
        hand_up(token)

    def announce(plane, carry):
        signal(ready, {"tm": at_plane(plane, 0)})
        return carry

    lax.fori_loop(1, z, announce, 0)

    @pl.when((z == 0) & (y == 0) & (space == 0))
    def _():
        for far in range(2 * HALF, 2 * DEPTH):
            signal(token_0, {"tm": tm + far})

    @pl.when(z > 0)
    def _():
        pl.semaphore_wait(token_0, 1)

    @pl.when((y == 1) & ((z < HALF - 1) | ((space > 0) & (z < DEPTH - 1))))
    def _():
        hand_up(token_0)

    @pl.when(z > 0)
    def _():
        signal(ready, {"tm": at_plane(0, 0)})

    cond_rows[...] = swap_blocks(cond_v[group])
    own_cond[...] = jnp.broadcast_to(cond_rows[pl.ds(rank, 1)], (LANES, LANES)).T

    row = lax.broadcasted_iota(jnp.int32, (8, LANES), 0)
    lane = lax.broadcasted_iota(jnp.int32, (8, LANES), 1)
    loads[3].wait()
    for copy in near[:2]:
        copy.wait_recv()

    def around(field, i, low, high):
        centre = field[i // 3, i % 3]
        low = jnp.broadcast_to(jnp.where(space == 0, 0.0, low), (8, LANES))
        high = jnp.broadcast_to(jnp.where(space == 7, 0.0, high), (8, LANES))
        z_low = jnp.where(row == 0, low, pltpu.roll(centre, 1, 0))
        z_high = jnp.where(row == 7, high, pltpu.roll(centre, 7, 0))
        y_low = jnp.where(lane == 0, 0.0, pltpu.roll(centre, 1, 1))
        y_high = jnp.where(lane == LANES - 1, 0.0, pltpu.roll(centre, LANES - 1, 1))
        total = (z_low + z_high) + (y_low + y_high)
        if i > 0:
            total += field[(i - 1) // 3, (i - 1) % 3]
        if i < ROWS - 1:
            total += field[(i + 1) // 3, (i + 1) % 3]
        return total

    mine = pl.ds(pl.multiple_of(2 * tm, 2), 2)

    def serve(plane, first):
        for j in range(first, 8):
            peer = at_plane(plane, j)
            theirs = pl.ds(pl.multiple_of(2 * peer, 2), 2)
            send(blocks.at[theirs], got.at[mine], block_send, block_recv, {"tm": peer})

    def serve_plane(plane, carry):
        serve(plane, 0)
        return carry

    def serve_lower(plane, carry):
        @pl.when(plane < z)
        def _():
            serve(plane, 0)

        return carry

    for i in range(ROWS):
        at = (i // 3, i % 3)
        s, p, w, cond = s_v[at], p_v[at], w_v[at], cond_v[i]
        around_s = around(s_v, i, from_low[i : i + 1], from_high[i : i + 1])
        around_w = around(
            w_v, i, from_low[ROWS + i : ROWS + i + 1], from_high[ROWS + i : ROWS + i + 1]
        )
        rs_ref[i] = s + diffusion * (cond * (6.0 * s - around_s)) - control_cost * p
        rp_ref[i] = p + diffusion * (6.0 * w - around_w) + tracking * (s - target_v[i])

    for q in range(3):
        for copy in near[2 + 2 * q : 4 + 2 * q]:
            copy.wait_recv()
        for i in range(q, ROWS, 3):
            rs = rs_ref[i] - s_prev[i // 3, q]
            rp = rp_ref[i] - p_next[i // 3, q]
            rs_ref[i] = rs
            rp_ref[i] = rp
            blocks[pl.ds(16 * i, 8, stride=2)] = swap_blocks(rs)
            blocks[pl.ds(16 * i + 1, 8, stride=2)] = swap_blocks(rp)
        lax.fori_loop(4 * q, 4 * q + 4, serve_lower, 0)

        @pl.when(lax.div(z, 4) == q)
        def _():
            serve(z, 1)

    own = pltpu.make_async_copy(blocks.at[mine], got.at[mine], block_recv)
    own.start()

    @pl.when(z < DEPTH - 1)
    def _():
        pl.semaphore_wait(ready, DEPTH - 1 - z)

    lax.fori_loop(z + 1, DEPTH, serve_plane, 0)
    for load in loads[4:]:
        load.wait()
    pltpu.make_async_copy(got, got, block_recv).wait()
    sent = blocks.at[pl.ds(0, TERMS - 2)]
    pltpu.make_async_copy(sent, sent, block_send).wait()
    for copy in near:
        copy.wait_send()


def solve(
    rs_ref, rp_ref, got, own_cond, high_v, low_v, trig_v,
    rs_hbm, rp_hbm, spec_hbm,
    spec_v, sem,
):
    copies = [
        pltpu.make_async_copy(rs_ref, rs_hbm, sem.at[0]),
        pltpu.make_async_copy(rp_ref, rp_hbm, sem.at[1]),
    ]
    for copy in copies:
        copy.start()
    def product(values, table):
        return lax.dot_general(
            values, table, (((0,), (0,)), ((), ())), preferred_element_type=jnp.float32
        )

    values = got[...]
    high = values.astype(jnp.bfloat16)
    low = (values - high.astype(jnp.float32)).astype(jnp.bfloat16)
    spectra = product(high, high_v[...]) + (product(high, low_v[...]) + product(low, high_v[...]))
    state_real, state_imag, adjoint_real, adjoint_imag = (
        spectra[:, LANES * i : LANES * (i + 1)] for i in range(4)
    )
    cosine, sine = trig_v[0:1], trig_v[1:2]
    diagonal = 1.0 + diffusion * 6.0 * own_cond[...] - cosine
    scale = 1.0 / (diagonal * diagonal + sine * sine + control_cost * tracking)
    fixes = (
        diagonal * state_real + sine * state_imag + control_cost * adjoint_real,
        diagonal * state_imag - sine * state_real + control_cost * adjoint_imag,
        diagonal * adjoint_real - sine * adjoint_imag - tracking * state_real,
        diagonal * adjoint_imag + sine * adjoint_real - tracking * state_imag,
    )
    for i, fix in enumerate(fixes):
        spec_v[i] = (fix * scale)[:, :STEPS]
        copy = pltpu.make_async_copy(spec_v.at[i], spec_hbm.at[i], sem.at[2 + i])
        copy.start()
        copies.append(copy)
    for copy in copies:
        copy.wait()


def shards(state_field, adjoint, target, conductivity):
    high, low, trig = dft_table()
    tiles = (ROWS, 8, LANES)
    parts = (ROWS // 3, 3, 8, LANES)
    stay = lambda array: pltpu.with_memory_space_constraint(array, pltpu.HBM)
    rows_first = lambda field: stay(jnp.transpose(field[0], (1, 0, 2)))
    in_parts = lambda field: stay(jnp.transpose(field[0], (1, 0, 2)).reshape(parts))
    vmem, dma = pltpu.VMEM, pltpu.SemaphoreType.DMA
    f32 = jnp.float32
    in_hbm = pl.BlockSpec(memory_space=pltpu.HBM)
    in_vmem = pl.BlockSpec(memory_space=pltpu.VMEM)
    rs, rp, got, own_cond, high, low, trig = pl.pallas_call(
        kernel,
        out_shape=(
            jax.ShapeDtypeStruct(tiles, f32),
            jax.ShapeDtypeStruct(tiles, f32),
            jax.ShapeDtypeStruct((TERMS, LANES), f32),
            jax.ShapeDtypeStruct((LANES, LANES), f32),
            jax.ShapeDtypeStruct((TERMS, 4 * LANES), jnp.bfloat16),
            jax.ShapeDtypeStruct((TERMS, 4 * LANES), jnp.bfloat16),
            jax.ShapeDtypeStruct((8, LANES), f32),
        ),
        in_specs=[in_hbm] * 7,
        out_specs=(in_vmem,) * 7,
        scratch_shapes=[
            vmem(parts, f32),
            vmem(parts, f32),
            vmem(parts, f32),
            vmem(tiles, f32),
            vmem(tiles, f32),
            vmem(parts, f32),
            vmem(parts, f32),
            vmem((2 * ROWS, LANES), f32),
            vmem((2 * ROWS, LANES), f32),
            vmem((2 * ROWS, LANES), f32),
            vmem((2 * ROWS, LANES), f32),
            vmem((TERMS, LANES), f32),
            vmem((8, LANES), f32),
            dma((7,)),
            dma((8,)),
            dma((8,)),
            dma,
            dma,
            pltpu.SemaphoreType.REGULAR,
            pltpu.SemaphoreType.REGULAR,
            pltpu.SemaphoreType.REGULAR,
        ],
        compiler_params=pltpu.CompilerParams(
            collective_id=0, has_side_effects=True, vmem_limit_bytes=24 * 1024 * 1024
        ),
    )(
        in_parts(state_field), in_parts(adjoint), rows_first(target),
        stay(jnp.transpose(conductivity, (1, 0, 2))),
        stay(jnp.asarray(high)), stay(jnp.asarray(low)), stay(jnp.asarray(trig)),
    )
    rs, rp, spec = pl.pallas_call(
        solve,
        out_shape=(
            jax.ShapeDtypeStruct(tiles, f32),
            jax.ShapeDtypeStruct(tiles, f32),
            jax.ShapeDtypeStruct((4, LANES, STEPS), f32),
        ),
        in_specs=[in_vmem] * 7,
        out_specs=(in_hbm,) * 3,
        scratch_shapes=[vmem((4, LANES, STEPS), f32), dma((6,))],
        compiler_params=pltpu.CompilerParams(vmem_limit_bytes=16 * 1024 * 1024),
    )(rs, rp, got, own_cond, high, low, trig)
    back = lambda tile: jnp.transpose(tile, (1, 0, 2))[None]
    spectral = jnp.transpose(spec.reshape(4, 8, BLOCK, STEPS), (0, 3, 1, 2))
    return back(rs), back(rp), spectral


def solution(mesh):
    placed = (
        P("tm", "space", None, None),
        P("tm", "space", None, None),
        P("tm", "space", None, None),
        P("space", None, None),
    )
    return jax.shard_map(
        shards,
        mesh=mesh,
        in_specs=placed,
        out_specs=(
            P("tm", "space", None, None),
            P("tm", "space", None, None),
            P(None, None, "space", "tm"),
        ),
        check_vma=False,
    )
```

```python
import functools
import math

import jax
import jax.numpy as jnp
import numpy as np
from jax import lax
from jax.experimental import pallas as pl
from jax.experimental.pallas import tpu as pltpu
from jax.sharding import PartitionSpec as P

diffusion = 0.05
control_cost = 0.2
tracking = 0.5

STEPS = 96
DEPTH = 12
HALF = 8
ROWS = 12
OWNERS = 8
BLOCK = 16
TERMS = 2 * STEPS
LANES = 128


def dft_table():
    times = np.arange(STEPS)
    angles = (np.outer(times, times) % STEPS) * (2.0 * math.pi / STEPS)
    table = np.zeros((STEPS, 2, 4, LANES))
    for field in range(2):
        table[:, field, 2 * field, :STEPS] = np.cos(angles)
        table[:, field, 2 * field + 1, :STEPS] = -np.sin(angles)
    table = table.reshape(2 * STEPS, 4 * LANES) / math.sqrt(STEPS)
    trig = np.zeros((8, LANES))
    trig[0, :STEPS] = np.cos(times * (2.0 * math.pi / STEPS))
    trig[1, :STEPS] = np.sin(times * (2.0 * math.pi / STEPS))
    table = table.astype(np.float32)
    high = table.astype(jnp.bfloat16)
    return high, (table - high.astype(np.float32)).astype(jnp.bfloat16), trig.astype(np.float32)


def swap_blocks(tile):
    row = lax.broadcasted_iota(jnp.int32, (8, LANES), 0)
    block = lax.broadcasted_iota(jnp.int32, (8, LANES), 1) // BLOCK
    for bit in (1, 2, 4):
        row_set = (row & bit) != 0
        block_set = (block & bit) != 0
        up = pltpu.roll(pltpu.roll(tile, 8 - bit, 0), BLOCK * bit, 1)
        if bit == 4:
            tile = jnp.where(row_set == block_set, tile, up)
        else:
            down = pltpu.roll(pltpu.roll(tile, bit, 0), LANES - BLOCK * bit, 1)
            tile = jnp.where(row_set == block_set, tile, jnp.where(block_set, up, down))
    return tile


def kernel(
    s_hbm, p_hbm, target_hbm, cond_hbm, high_hbm, low_hbm, trig_hbm,
    rs_ref, rp_ref, got, own_cond, high_v, low_v, trig_v,
    s_v, p_v, w_v, target_v, cond_v,
    s_prev, p_next, edge_low, edge_high, from_low, from_high,
    blocks, cond_rows,
    load_sem, near_send, near_recv, block_send, block_recv, token, token_0, ready,
):
    tm = lax.axis_index("tm")
    space = lax.axis_index("space")
    group = lax.div(tm, OWNERS)
    rank = lax.rem(tm, OWNERS)
    later = lax.rem(tm + 1, STEPS)
    earlier = lax.rem(tm + STEPS - 1, STEPS)
    above = lax.rem(space + 1, 8)
    below = lax.rem(space + 7, 8)

    loads = [
        pltpu.make_async_copy(source, target, load_sem.at[i])
        for i, (source, target) in enumerate(
            (
                (s_hbm, s_v),
                (p_hbm, p_v),
                (cond_hbm, cond_v),
                (target_hbm, target_v),
                (high_hbm, high_v),
                (low_hbm, low_v),
                (trig_hbm, trig_v),
            )
        )
    ]
    x, y, z = lax.div(tm, 2 * DEPTH), lax.rem(tm, 2), lax.rem(lax.div(tm, 2), DEPTH)

    def at_plane(plane, j):
        return 2 * DEPTH * lax.rem(x + j // 2, 4) + 2 * plane + lax.rem(y + j, 2)

    def signal(semaphore, where):
        pl.semaphore_signal(semaphore, 1, device_id=where, device_id_type=pl.DeviceIdType.MESH)

    barrier = pltpu.get_barrier_semaphore()
    signal(barrier, {"space": above})
    signal(barrier, {"space": below})
    signal(barrier, {"tm": lax.rem(tm + STEPS - 1 + 2 * y, STEPS)})
    for j in range(1, 8):
        signal(barrier, {"tm": at_plane(z, j)})

    @pl.when(z > 0)
    def _():
        signal(barrier, {"tm": tm - 2})

    @pl.when(z < DEPTH - 1)
    def _():
        signal(barrier, {"tm": tm + 2})

    @pl.when((z >= HALF) & (space == 0))
    def _():
        signal(barrier, {"tm": 2 * DEPTH * x})

    @pl.when((z == 0) & (y == 0) & (space == 0))
    def _():
        for far in range(2 * HALF, 2 * DEPTH):
            signal(barrier, {"tm": tm + far})

    for load in loads:
        load.start()

    for load in loads[:3]:
        load.wait()
    for i in range(ROWS):
        w_v[i // 3, i % 3] = cond_v[i] * p_v[i // 3, i % 3]
    for edge, plane in ((edge_low, 0), (edge_high, 7)):
        for i in range(ROWS):
            edge[i : i + 1] = s_v[i // 3, i % 3, plane : plane + 1]
            edge[ROWS + i : ROWS + i + 1] = w_v[i // 3, i % 3, plane : plane + 1]

    last = DEPTH - 1
    greetings = 10 + (z + last - 1) // last + (2 * last - 1 - z) // last
    wrapped = (z + last - HALF) // last + 2 * (DEPTH - HALF) * (1 - y) * ((last - z) // last)
    greetings += wrapped * (1 - (space + 7) // 8)
    pl.semaphore_wait(barrier, greetings)

    @pl.when((z == 0) & (y == 0) & (space == 0))
    def _():
        for far in range(2 * HALF, 2 * DEPTH):
            signal(token_0, {"tm": tm + far})

    def send(source, target, send_sem, recv_sem, where):
        copy = pltpu.make_async_remote_copy(
            src_ref=source, dst_ref=target, send_sem=send_sem, recv_sem=recv_sem,
            device_id=where, device_id_type=pl.DeviceIdType.MESH,
        )
        copy.start()
        return copy

    def send_part(q):
        part, k = (slice(None), q), 2 + 2 * q
        return [
            send(s_v.at[part], s_prev.at[part], near_send.at[k], near_recv.at[k], {"tm": later}),
            send(p_v.at[part], p_next.at[part], near_send.at[k + 1], near_recv.at[k + 1],
                 {"tm": earlier}),
        ]

    first_part = send_part(0)
    near = [
        send(edge_low, from_high, near_send.at[0], near_recv.at[0], {"space": below}),
        send(edge_high, from_low, near_send.at[1], near_recv.at[1], {"space": above}),
    ] + first_part + send_part(1) + send_part(2)

    @pl.when(z > 1)
    def _():
        pl.semaphore_wait(token, 1)

    def hand_up(semaphore):
        signal(semaphore, {"tm": tm + 2})
        signal(semaphore, {"tm": tm + 1})

    @pl.when((y == 1) & (z > 0) & (z < DEPTH - 1))
    def _():
        hand_up(token)

    def announce(plane, carry):
        signal(ready, {"tm": at_plane(plane, 0)})
        return carry

    lax.fori_loop(1, z, announce, 0)

    @pl.when(z > 0)
    def _():
        pl.semaphore_wait(token_0, 1)

    @pl.when((y == 1) & ((z < HALF - 1) | ((space > 0) & (z < DEPTH - 1))))
    def _():
        hand_up(token_0)

    @pl.when(z > 0)
    def _():
        signal(ready, {"tm": at_plane(0, 0)})

    cond_rows[...] = swap_blocks(cond_v[group])
    own_cond[...] = jnp.broadcast_to(cond_rows[pl.ds(rank, 1)], (LANES, LANES)).T

    row = lax.broadcasted_iota(jnp.int32, (8, LANES), 0)
    lane = lax.broadcasted_iota(jnp.int32, (8, LANES), 1)
    loads[3].wait()
    for copy in near[:2]:
        copy.wait_recv()

    def around(field, i, low, high):
        centre = field[i // 3, i % 3]
        low = jnp.broadcast_to(jnp.where(space == 0, 0.0, low), (8, LANES))
        high = jnp.broadcast_to(jnp.where(space == 7, 0.0, high), (8, LANES))
        z_low = jnp.where(row == 0, low, pltpu.roll(centre, 1, 0))
        z_high = jnp.where(row == 7, high, pltpu.roll(centre, 7, 0))
        y_low = jnp.where(lane == 0, 0.0, pltpu.roll(centre, 1, 1))
        y_high = jnp.where(lane == LANES - 1, 0.0, pltpu.roll(centre, LANES - 1, 1))
        total = (z_low + z_high) + (y_low + y_high)
        if i > 0:
            total += field[(i - 1) // 3, (i - 1) % 3]
        if i < ROWS - 1:
            total += field[(i + 1) // 3, (i + 1) % 3]
        return total

    mine = pl.ds(pl.multiple_of(2 * tm, 2), 2)

    def serve(plane, first):
        for j in range(first, 8):
            peer = at_plane(plane, j)
            theirs = pl.ds(pl.multiple_of(2 * peer, 2), 2)
            send(blocks.at[theirs], got.at[mine], block_send, block_recv, {"tm": peer})

    def serve_plane(plane, carry):
        serve(plane, 0)
        return carry

    def serve_lower(plane, carry):
        @pl.when(plane < z)
        def _():
            serve(plane, 0)

        return carry

    for i in range(ROWS):
        at = (i // 3, i % 3)
        s, p, w, cond = s_v[at], p_v[at], w_v[at], cond_v[i]
        around_s = around(s_v, i, from_low[i : i + 1], from_high[i : i + 1])
        around_w = around(
            w_v, i, from_low[ROWS + i : ROWS + i + 1], from_high[ROWS + i : ROWS + i + 1]
        )
        rs_ref[i] = s + diffusion * (cond * (6.0 * s - around_s)) - control_cost * p
        rp_ref[i] = p + diffusion * (6.0 * w - around_w) + tracking * (s - target_v[i])

    for q in range(3):
        for copy in near[2 + 2 * q : 4 + 2 * q]:
            copy.wait_recv()
        for i in range(q, ROWS, 3):
            rs = rs_ref[i] - s_prev[i // 3, q]
            rp = rp_ref[i] - p_next[i // 3, q]
            rs_ref[i] = rs
            rp_ref[i] = rp
            blocks[pl.ds(16 * i, 8, stride=2)] = swap_blocks(rs)
            blocks[pl.ds(16 * i + 1, 8, stride=2)] = swap_blocks(rp)
        lax.fori_loop(4 * q, 4 * q + 4, serve_lower, 0)

        @pl.when(lax.div(z, 4) == q)
        def _():
            serve(z, 1)

    own = pltpu.make_async_copy(blocks.at[mine], got.at[mine], block_recv)
    own.start()

    @pl.when(z < DEPTH - 1)
    def _():
        pl.semaphore_wait(ready, DEPTH - 1 - z)

    lax.fori_loop(z + 1, DEPTH, serve_plane, 0)
    for load in loads[4:]:
        load.wait()
    pltpu.make_async_copy(got, got, block_recv).wait()
    sent = blocks.at[pl.ds(0, TERMS - 2)]
    pltpu.make_async_copy(sent, sent, block_send).wait()
    for copy in near:
        copy.wait_send()


def solve(
    rs_ref, rp_ref, got, own_cond, high_v, low_v, trig_v,
    rs_hbm, rp_hbm, spec_hbm,
    spec_v, sem,
):
    copies = [
        pltpu.make_async_copy(rs_ref, rs_hbm, sem.at[0]),
        pltpu.make_async_copy(rp_ref, rp_hbm, sem.at[1]),
    ]
    for copy in copies:
        copy.start()
    def product(values, table):
        return lax.dot_general(
            values, table, (((0,), (0,)), ((), ())), preferred_element_type=jnp.float32
        )

    values = got[...]
    high = values.astype(jnp.bfloat16)
    low = (values - high.astype(jnp.float32)).astype(jnp.bfloat16)
    spectra = product(high, high_v[...]) + (product(high, low_v[...]) + product(low, high_v[...]))
    state_real, state_imag, adjoint_real, adjoint_imag = (
        spectra[:, LANES * i : LANES * (i + 1)] for i in range(4)
    )
    cosine, sine = trig_v[0:1], trig_v[1:2]
    diagonal = 1.0 + diffusion * 6.0 * own_cond[...] - cosine
    scale = 1.0 / (diagonal * diagonal + sine * sine + control_cost * tracking)
    fixes = (
        diagonal * state_real + sine * state_imag + control_cost * adjoint_real,
        diagonal * state_imag - sine * state_real + control_cost * adjoint_imag,
        diagonal * adjoint_real - sine * adjoint_imag - tracking * state_real,
        diagonal * adjoint_imag + sine * adjoint_real - tracking * state_imag,
    )
    for i, fix in enumerate(fixes):
        spec_v[i] = (fix * scale)[:, :STEPS]
        copy = pltpu.make_async_copy(spec_v.at[i], spec_hbm.at[i], sem.at[2 + i])
        copy.start()
        copies.append(copy)
    for copy in copies:
        copy.wait()


def shards(state_field, adjoint, target, conductivity):
    high, low, trig = dft_table()
    tiles = (ROWS, 8, LANES)
    parts = (ROWS // 3, 3, 8, LANES)
    stay = lambda array: pltpu.with_memory_space_constraint(array, pltpu.HBM)
    rows_first = lambda field: stay(jnp.transpose(field[0], (1, 0, 2)))
    in_parts = lambda field: stay(jnp.transpose(field[0], (1, 0, 2)).reshape(parts))
    vmem, dma = pltpu.VMEM, pltpu.SemaphoreType.DMA
    f32 = jnp.float32
    in_hbm = pl.BlockSpec(memory_space=pltpu.HBM)
    in_vmem = pl.BlockSpec(memory_space=pltpu.VMEM)
    rs, rp, got, own_cond, high, low, trig = pl.pallas_call(
        kernel,
        out_shape=(
            jax.ShapeDtypeStruct(tiles, f32),
            jax.ShapeDtypeStruct(tiles, f32),
            jax.ShapeDtypeStruct((TERMS, LANES), f32),
            jax.ShapeDtypeStruct((LANES, LANES), f32),
            jax.ShapeDtypeStruct((TERMS, 4 * LANES), jnp.bfloat16),
            jax.ShapeDtypeStruct((TERMS, 4 * LANES), jnp.bfloat16),
            jax.ShapeDtypeStruct((8, LANES), f32),
        ),
        in_specs=[in_hbm] * 7,
        out_specs=(in_vmem,) * 7,
        scratch_shapes=[
            vmem(parts, f32),
            vmem(parts, f32),
            vmem(parts, f32),
            vmem(tiles, f32),
            vmem(tiles, f32),
            vmem(parts, f32),
            vmem(parts, f32),
            vmem((2 * ROWS, LANES), f32),
            vmem((2 * ROWS, LANES), f32),
            vmem((2 * ROWS, LANES), f32),
            vmem((2 * ROWS, LANES), f32),
            vmem((TERMS, LANES), f32),
            vmem((8, LANES), f32),
            dma((7,)),
            dma((8,)),
            dma((8,)),
            dma,
            dma,
            pltpu.SemaphoreType.REGULAR,
            pltpu.SemaphoreType.REGULAR,
            pltpu.SemaphoreType.REGULAR,
        ],
        compiler_params=pltpu.CompilerParams(
            collective_id=0, has_side_effects=True, vmem_limit_bytes=24 * 1024 * 1024
        ),
    )(
        in_parts(state_field), in_parts(adjoint), rows_first(target),
        stay(jnp.transpose(conductivity, (1, 0, 2))),
        stay(jnp.asarray(high)), stay(jnp.asarray(low)), stay(jnp.asarray(trig)),
    )
    rs, rp, spec = pl.pallas_call(
        solve,
        out_shape=(
            jax.ShapeDtypeStruct(tiles, f32),
            jax.ShapeDtypeStruct(tiles, f32),
            jax.ShapeDtypeStruct((4, LANES, STEPS), f32),
        ),
        in_specs=[in_vmem] * 7,
        out_specs=(in_hbm,) * 3,
        scratch_shapes=[vmem((4, LANES, STEPS), f32), dma((6,))],
        compiler_params=pltpu.CompilerParams(vmem_limit_bytes=16 * 1024 * 1024),
    )(rs, rp, got, own_cond, high, low, trig)
    back = lambda tile: jnp.transpose(tile, (1, 0, 2))[None]
    spectral = jnp.transpose(spec.reshape(4, 8, BLOCK, STEPS), (0, 3, 1, 2))
    return back(rs), back(rp), spectral


def solution(mesh):
    placed = (
        P("tm", "space", None, None),
        P("tm", "space", None, None),
        P("tm", "space", None, None),
        P("space", None, None),
    )
    return jax.shard_map(
        shards,
        mesh=mesh,
        in_specs=placed,
        out_specs=(
            P("tm", "space", None, None),
            P("tm", "space", None, None),
            P(None, None, "space", "tm"),
        ),
        check_vma=False,
    )
```

```python
import functools
import math

import jax
import jax.numpy as jnp
import numpy as np
from jax import lax
from jax.experimental import pallas as pl
from jax.experimental.pallas import tpu as pltpu
from jax.sharding import PartitionSpec as P

diffusion = 0.05
control_cost = 0.2
tracking = 0.5

STEPS = 96
DEPTH = 12
HALF = 8
ROWS = 12
OWNERS = 8
BLOCK = 16
TERMS = 2 * STEPS
LANES = 128


def dft_table():
    times = np.arange(STEPS)
    angles = (np.outer(times, times) % STEPS) * (2.0 * math.pi / STEPS)
    table = np.zeros((STEPS, 2, 4, LANES))
    for field in range(2):
        table[:, field, 2 * field, :STEPS] = np.cos(angles)
        table[:, field, 2 * field + 1, :STEPS] = -np.sin(angles)
    table = table.reshape(2 * STEPS, 4 * LANES) / math.sqrt(STEPS)
    trig = np.zeros((8, LANES))
    trig[0, :STEPS] = np.cos(times * (2.0 * math.pi / STEPS))
    trig[1, :STEPS] = np.sin(times * (2.0 * math.pi / STEPS))
    table = table.astype(np.float32)
    high = table.astype(jnp.bfloat16)
    return high, (table - high.astype(np.float32)).astype(jnp.bfloat16), trig.astype(np.float32)


def swap_blocks(tile):
    row = lax.broadcasted_iota(jnp.int32, (8, LANES), 0)
    block = lax.broadcasted_iota(jnp.int32, (8, LANES), 1) // BLOCK
    for bit in (1, 2, 4):
        row_set = (row & bit) != 0
        block_set = (block & bit) != 0
        up = pltpu.roll(pltpu.roll(tile, 8 - bit, 0), BLOCK * bit, 1)
        if bit == 4:
            tile = jnp.where(row_set == block_set, tile, up)
        else:
            down = pltpu.roll(pltpu.roll(tile, bit, 0), LANES - BLOCK * bit, 1)
            tile = jnp.where(row_set == block_set, tile, jnp.where(block_set, up, down))
    return tile


def kernel(
    s_hbm, p_hbm, target_hbm, cond_hbm, high_hbm, low_hbm, trig_hbm,
    rs_ref, rp_ref, got, own_cond, high_v, low_v, trig_v,
    s_v, p_v, w_v, target_v, cond_v,
    s_prev, p_next, edge_low, edge_high, from_low, from_high,
    blocks, cond_rows,
    load_sem, near_send, near_recv, block_send, block_recv, token, token_0, ready,
):
    tm = lax.axis_index("tm")
    space = lax.axis_index("space")
    group = lax.div(tm, OWNERS)
    rank = lax.rem(tm, OWNERS)
    later = lax.rem(tm + 1, STEPS)
    earlier = lax.rem(tm + STEPS - 1, STEPS)
    above = lax.rem(space + 1, 8)
    below = lax.rem(space + 7, 8)

    loads = [
        pltpu.make_async_copy(source, target, load_sem.at[i])
        for i, (source, target) in enumerate(
            (
                (s_hbm, s_v),
                (p_hbm, p_v),
                (cond_hbm, cond_v),
                (target_hbm, target_v),
                (high_hbm, high_v),
                (low_hbm, low_v),
                (trig_hbm, trig_v),
            )
        )
    ]
    x, y, z = lax.div(tm, 2 * DEPTH), lax.rem(tm, 2), lax.rem(lax.div(tm, 2), DEPTH)

    def at_plane(plane, j):
        return 2 * DEPTH * lax.rem(x + j // 2, 4) + 2 * plane + lax.rem(y + j, 2)

    def signal(semaphore, where):
        pl.semaphore_signal(semaphore, 1, device_id=where, device_id_type=pl.DeviceIdType.MESH)

    barrier = pltpu.get_barrier_semaphore()
    signal(barrier, {"space": above})
    signal(barrier, {"space": below})
    signal(barrier, {"tm": lax.rem(tm + STEPS - 1 + 2 * y, STEPS)})
    for j in range(1, 8):
        signal(barrier, {"tm": at_plane(z, j)})

    @pl.when(z > 0)
    def _():
        signal(barrier, {"tm": tm - 2})

    @pl.when(z < DEPTH - 1)
    def _():
        signal(barrier, {"tm": tm + 2})

    @pl.when((z >= HALF) & (space == 0))
    def _():
        signal(barrier, {"tm": 2 * DEPTH * x})

    @pl.when((z == 0) & (y == 0) & (space == 0))
    def _():
        for far in range(2 * HALF, 2 * DEPTH):
            signal(barrier, {"tm": tm + far})

    for load in loads:
        load.start()

    for load in loads[:3]:
        load.wait()
    for i in range(ROWS):
        w_v[i // 3, i % 3] = cond_v[i] * p_v[i // 3, i % 3]
    for edge, plane in ((edge_low, 0), (edge_high, 7)):
        for i in range(ROWS):
            edge[i : i + 1] = s_v[i // 3, i % 3, plane : plane + 1]
            edge[ROWS + i : ROWS + i + 1] = w_v[i // 3, i % 3, plane : plane + 1]

    last = DEPTH - 1
    greetings = 10 + (z + last - 1) // last + (2 * last - 1 - z) // last
    wrapped = (z + last - HALF) // last + 2 * (DEPTH - HALF) * (1 - y) * ((last - z) // last)
    greetings += wrapped * (1 - (space + 7) // 8)
    pl.semaphore_wait(barrier, greetings)

    @pl.when((z == 0) & (y == 0) & (space == 0))
    def _():
        for far in range(2 * HALF, 2 * DEPTH):
            signal(token_0, {"tm": tm + far})

    def send(source, target, send_sem, recv_sem, where):
        copy = pltpu.make_async_remote_copy(
            src_ref=source, dst_ref=target, send_sem=send_sem, recv_sem=recv_sem,
            device_id=where, device_id_type=pl.DeviceIdType.MESH,
        )
        copy.start()
        return copy

    def send_part(q):
        part, k = (slice(None), q), 2 + 2 * q
        return [
            send(s_v.at[part], s_prev.at[part], near_send.at[k], near_recv.at[k], {"tm": later}),
            send(p_v.at[part], p_next.at[part], near_send.at[k + 1], near_recv.at[k + 1],
                 {"tm": earlier}),
        ]

    first_part = send_part(0)
    near = [
        send(edge_low, from_high, near_send.at[0], near_recv.at[0], {"space": below}),
        send(edge_high, from_low, near_send.at[1], near_recv.at[1], {"space": above}),
    ] + first_part + send_part(1) + send_part(2)

    @pl.when(z > 1)
    def _():
        pl.semaphore_wait(token, 1)

    def hand_up(semaphore):
        signal(semaphore, {"tm": tm + 2})
        signal(semaphore, {"tm": tm + 1})

    @pl.when((y == 1) & (z > 0) & (z < DEPTH - 1))
    def _():
        hand_up(token)

    @pl.when(z > 0)
    def _():
        pl.semaphore_wait(token_0, 1)

    @pl.when((y == 1) & ((z < HALF - 1) | ((space > 0) & (z < DEPTH - 1))))
    def _():
        hand_up(token_0)

    @pl.when(z > 0)
    def _():
        signal(ready, {"tm": at_plane(0, 0)})

    def announce(plane, carry):
        signal(ready, {"tm": at_plane(plane, 0)})
        return carry

    lax.fori_loop(1, z, announce, 0)

    cond_rows[...] = swap_blocks(cond_v[group])
    own_cond[...] = jnp.broadcast_to(cond_rows[pl.ds(rank, 1)], (LANES, LANES)).T

    row = lax.broadcasted_iota(jnp.int32, (8, LANES), 0)
    lane = lax.broadcasted_iota(jnp.int32, (8, LANES), 1)
    loads[3].wait()
    for copy in near[:2]:
        copy.wait_recv()

    def around(field, i, low, high):
        centre = field[i // 3, i % 3]
        low = jnp.broadcast_to(jnp.where(space == 0, 0.0, low), (8, LANES))
        high = jnp.broadcast_to(jnp.where(space == 7, 0.0, high), (8, LANES))
        z_low = jnp.where(row == 0, low, pltpu.roll(centre, 1, 0))
        z_high = jnp.where(row == 7, high, pltpu.roll(centre, 7, 0))
        y_low = jnp.where(lane == 0, 0.0, pltpu.roll(centre, 1, 1))
        y_high = jnp.where(lane == LANES - 1, 0.0, pltpu.roll(centre, LANES - 1, 1))
        total = (z_low + z_high) + (y_low + y_high)
        if i > 0:
            total += field[(i - 1) // 3, (i - 1) % 3]
        if i < ROWS - 1:
            total += field[(i + 1) // 3, (i + 1) % 3]
        return total

    mine = pl.ds(pl.multiple_of(2 * tm, 2), 2)

    def serve(plane, first):
        for j in (5, 4, 7, 3, 6, 2, 1, 0)[: 8 - first]:
            peer = at_plane(plane, j)
            theirs = pl.ds(pl.multiple_of(2 * peer, 2), 2)
            send(blocks.at[theirs], got.at[mine], block_send, block_recv, {"tm": peer})

    def serve_plane(plane, carry):
        serve(plane, 0)
        return carry

    def serve_lower(plane, carry):
        @pl.when(plane < z)
        def _():
            serve(plane, 0)

        return carry

    for i in range(ROWS):
        at = (i // 3, i % 3)
        s, p, w, cond = s_v[at], p_v[at], w_v[at], cond_v[i]
        around_s = around(s_v, i, from_low[i : i + 1], from_high[i : i + 1])
        around_w = around(
            w_v, i, from_low[ROWS + i : ROWS + i + 1], from_high[ROWS + i : ROWS + i + 1]
        )
        rs_ref[i] = s + diffusion * (cond * (6.0 * s - around_s)) - control_cost * p
        rp_ref[i] = p + diffusion * (6.0 * w - around_w) + tracking * (s - target_v[i])

    for q in range(3):
        for copy in near[2 + 2 * q : 4 + 2 * q]:
            copy.wait_recv()
        for i in range(q, ROWS, 3):
            rs = rs_ref[i] - s_prev[i // 3, q]
            rp = rp_ref[i] - p_next[i // 3, q]
            rs_ref[i] = rs
            rp_ref[i] = rp
            blocks[pl.ds(16 * i, 8, stride=2)] = swap_blocks(rs)
            blocks[pl.ds(16 * i + 1, 8, stride=2)] = swap_blocks(rp)
        lax.fori_loop(4 * q, 4 * q + 4, serve_lower, 0)

        @pl.when(lax.div(z, 4) == q)
        def _():
            serve(z, 1)

    own = pltpu.make_async_copy(blocks.at[mine], got.at[mine], block_recv)
    own.start()

    @pl.when(z < DEPTH - 1)
    def _():
        pl.semaphore_wait(ready, DEPTH - 1 - z)

    lax.fori_loop(z + 1, DEPTH, serve_plane, 0)
    for load in loads[4:]:
        load.wait()
    pltpu.make_async_copy(got, got, block_recv).wait()
    sent = blocks.at[pl.ds(0, TERMS - 2)]
    pltpu.make_async_copy(sent, sent, block_send).wait()
    for copy in near:
        copy.wait_send()


def solve(
    rs_ref, rp_ref, got, own_cond, high_v, low_v, trig_v,
    rs_hbm, rp_hbm, spec_hbm,
    spec_v, sem,
):
    copies = [
        pltpu.make_async_copy(rs_ref, rs_hbm, sem.at[0]),
        pltpu.make_async_copy(rp_ref, rp_hbm, sem.at[1]),
    ]
    for copy in copies:
        copy.start()
    def product(values, table):
        return lax.dot_general(
            values, table, (((0,), (0,)), ((), ())), preferred_element_type=jnp.float32
        )

    values = got[...]
    high = values.astype(jnp.bfloat16)
    low = (values - high.astype(jnp.float32)).astype(jnp.bfloat16)
    spectra = product(high, high_v[...]) + (product(high, low_v[...]) + product(low, high_v[...]))
    state_real, state_imag, adjoint_real, adjoint_imag = (
        spectra[:, LANES * i : LANES * (i + 1)] for i in range(4)
    )
    cosine, sine = trig_v[0:1], trig_v[1:2]
    diagonal = 1.0 + diffusion * 6.0 * own_cond[...] - cosine
    scale = 1.0 / (diagonal * diagonal + sine * sine + control_cost * tracking)
    fixes = (
        diagonal * state_real + sine * state_imag + control_cost * adjoint_real,
        diagonal * state_imag - sine * state_real + control_cost * adjoint_imag,
        diagonal * adjoint_real - sine * adjoint_imag - tracking * state_real,
        diagonal * adjoint_imag + sine * adjoint_real - tracking * state_imag,
    )
    for i, fix in enumerate(fixes):
        spec_v[i] = (fix * scale)[:, :STEPS]
        copy = pltpu.make_async_copy(spec_v.at[i], spec_hbm.at[i], sem.at[2 + i])
        copy.start()
        copies.append(copy)
    for copy in copies:
        copy.wait()


def shards(state_field, adjoint, target, conductivity):
    high, low, trig = dft_table()
    tiles = (ROWS, 8, LANES)
    parts = (ROWS // 3, 3, 8, LANES)
    stay = lambda array: pltpu.with_memory_space_constraint(array, pltpu.HBM)
    rows_first = lambda field: stay(jnp.transpose(field[0], (1, 0, 2)))
    in_parts = lambda field: stay(jnp.transpose(field[0], (1, 0, 2)).reshape(parts))
    vmem, dma = pltpu.VMEM, pltpu.SemaphoreType.DMA
    f32 = jnp.float32
    in_hbm = pl.BlockSpec(memory_space=pltpu.HBM)
    in_vmem = pl.BlockSpec(memory_space=pltpu.VMEM)
    rs, rp, got, own_cond, high, low, trig = pl.pallas_call(
        kernel,
        out_shape=(
            jax.ShapeDtypeStruct(tiles, f32),
            jax.ShapeDtypeStruct(tiles, f32),
            jax.ShapeDtypeStruct((TERMS, LANES), f32),
            jax.ShapeDtypeStruct((LANES, LANES), f32),
            jax.ShapeDtypeStruct((TERMS, 4 * LANES), jnp.bfloat16),
            jax.ShapeDtypeStruct((TERMS, 4 * LANES), jnp.bfloat16),
            jax.ShapeDtypeStruct((8, LANES), f32),
        ),
        in_specs=[in_hbm] * 7,
        out_specs=(in_vmem,) * 7,
        scratch_shapes=[
            vmem(parts, f32),
            vmem(parts, f32),
            vmem(parts, f32),
            vmem(tiles, f32),
            vmem(tiles, f32),
            vmem(parts, f32),
            vmem(parts, f32),
            vmem((2 * ROWS, LANES), f32),
            vmem((2 * ROWS, LANES), f32),
            vmem((2 * ROWS, LANES), f32),
            vmem((2 * ROWS, LANES), f32),
            vmem((TERMS, LANES), f32),
            vmem((8, LANES), f32),
            dma((7,)),
            dma((8,)),
            dma((8,)),
            dma,
            dma,
            pltpu.SemaphoreType.REGULAR,
            pltpu.SemaphoreType.REGULAR,
            pltpu.SemaphoreType.REGULAR,
        ],
        compiler_params=pltpu.CompilerParams(
            collective_id=0, has_side_effects=True, vmem_limit_bytes=24 * 1024 * 1024
        ),
    )(
        in_parts(state_field), in_parts(adjoint), rows_first(target),
        stay(jnp.transpose(conductivity, (1, 0, 2))),
        stay(jnp.asarray(high)), stay(jnp.asarray(low)), stay(jnp.asarray(trig)),
    )
    rs, rp, spec = pl.pallas_call(
        solve,
        out_shape=(
            jax.ShapeDtypeStruct(tiles, f32),
            jax.ShapeDtypeStruct(tiles, f32),
            jax.ShapeDtypeStruct((4, LANES, STEPS), f32),
        ),
        in_specs=[in_vmem] * 7,
        out_specs=(in_hbm,) * 3,
        scratch_shapes=[vmem((4, LANES, STEPS), f32), dma((6,))],
        compiler_params=pltpu.CompilerParams(vmem_limit_bytes=16 * 1024 * 1024),
    )(rs, rp, got, own_cond, high, low, trig)
    back = lambda tile: jnp.transpose(tile, (1, 0, 2))[None]
    spectral = jnp.transpose(spec.reshape(4, 8, BLOCK, STEPS), (0, 3, 1, 2))
    return back(rs), back(rp), spectral


def solution(mesh):
    placed = (
        P("tm", "space", None, None),
        P("tm", "space", None, None),
        P("tm", "space", None, None),
        P("space", None, None),
    )
    return jax.shard_map(
        shards,
        mesh=mesh,
        in_specs=placed,
        out_specs=(
            P("tm", "space", None, None),
            P("tm", "space", None, None),
            P(None, None, "space", "tm"),
        ),
        check_vma=False,
    )
```

```python
import functools
import math

import jax
import jax.numpy as jnp
import numpy as np
from jax import lax
from jax.experimental import pallas as pl
from jax.experimental.pallas import tpu as pltpu
from jax.sharding import PartitionSpec as P

diffusion = 0.05
control_cost = 0.2
tracking = 0.5

STEPS = 96
DEPTH = 12
HALF = 8
ROWS = 12
OWNERS = 8
BLOCK = 16
TERMS = 2 * STEPS
LANES = 128


def dft_table():
    times = np.arange(STEPS)
    angles = (np.outer(times, times) % STEPS) * (2.0 * math.pi / STEPS)
    table = np.zeros((STEPS, 2, 4, LANES))
    for field in range(2):
        table[:, field, 2 * field, :STEPS] = np.cos(angles)
        table[:, field, 2 * field + 1, :STEPS] = -np.sin(angles)
    table = table.reshape(2 * STEPS, 4 * LANES) / math.sqrt(STEPS)
    trig = np.zeros((8, LANES))
    trig[0, :STEPS] = np.cos(times * (2.0 * math.pi / STEPS))
    trig[1, :STEPS] = np.sin(times * (2.0 * math.pi / STEPS))
    table = table.astype(np.float32)
    high = table.astype(jnp.bfloat16)
    return high, (table - high.astype(np.float32)).astype(jnp.bfloat16), trig.astype(np.float32)


def swap_blocks(tile):
    row = lax.broadcasted_iota(jnp.int32, (8, LANES), 0)
    block = lax.broadcasted_iota(jnp.int32, (8, LANES), 1) // BLOCK
    for bit in (1, 2, 4):
        row_set = (row & bit) != 0
        block_set = (block & bit) != 0
        up = pltpu.roll(pltpu.roll(tile, 8 - bit, 0), BLOCK * bit, 1)
        if bit == 4:
            tile = jnp.where(row_set == block_set, tile, up)
        else:
            down = pltpu.roll(pltpu.roll(tile, bit, 0), LANES - BLOCK * bit, 1)
            tile = jnp.where(row_set == block_set, tile, jnp.where(block_set, up, down))
    return tile


def kernel(
    s_hbm, p_hbm, target_hbm, cond_hbm, high_hbm, low_hbm, trig_hbm,
    rs_ref, rp_ref, got, own_cond, high_v, low_v, trig_v,
    s_v, p_v, w_v, target_v, cond_v,
    s_prev, p_next, edge_low, edge_high, from_low, from_high,
    blocks, cond_rows,
    load_sem, near_send, near_recv, block_send, block_recv, token, token_0, ready,
):
    tm = lax.axis_index("tm")
    space = lax.axis_index("space")
    group = lax.div(tm, OWNERS)
    rank = lax.rem(tm, OWNERS)
    later = lax.rem(tm + 1, STEPS)
    earlier = lax.rem(tm + STEPS - 1, STEPS)
    above = lax.rem(space + 1, 8)
    below = lax.rem(space + 7, 8)

    loads = [
        pltpu.make_async_copy(source, target, load_sem.at[i])
        for i, (source, target) in enumerate(
            (
                (s_hbm, s_v),
                (p_hbm, p_v),
                (cond_hbm, cond_v),
                (target_hbm, target_v),
                (high_hbm, high_v),
                (low_hbm, low_v),
                (trig_hbm, trig_v),
            )
        )
    ]
    x, y, z = lax.div(tm, 2 * DEPTH), lax.rem(tm, 2), lax.rem(lax.div(tm, 2), DEPTH)

    def at_plane(plane, j):
        return 2 * DEPTH * lax.rem(x + j // 2, 4) + 2 * plane + lax.rem(y + j, 2)

    def signal(semaphore, where):
        pl.semaphore_signal(semaphore, 1, device_id=where, device_id_type=pl.DeviceIdType.MESH)

    barrier = pltpu.get_barrier_semaphore()
    signal(barrier, {"space": above})
    signal(barrier, {"space": below})
    signal(barrier, {"tm": lax.rem(tm + STEPS - 1 + 2 * y, STEPS)})
    for j in range(1, 8):
        signal(barrier, {"tm": at_plane(z, j)})

    @pl.when((y == 1) & (z > 0))
    def _():
        signal(barrier, {"tm": tm - 2})

    @pl.when((y == 1) & (z < DEPTH - 1))
    def _():
        signal(barrier, {"tm": tm + 2})

    @pl.when((z >= HALF) & (space == 0))
    def _():
        signal(barrier, {"tm": 2 * DEPTH * x})

    @pl.when((z == 0) & (y == 0) & (space == 0))
    def _():
        for far in range(2 * HALF, 2 * DEPTH):
            signal(barrier, {"tm": tm + far})

    for load in loads:
        load.start()

    for load in loads[:3]:
        load.wait()
    for i in range(ROWS):
        w_v[i // 3, i % 3] = cond_v[i] * p_v[i // 3, i % 3]
    for edge, plane in ((edge_low, 0), (edge_high, 7)):
        for i in range(ROWS):
            edge[i : i + 1] = s_v[i // 3, i % 3, plane : plane + 1]
            edge[ROWS + i : ROWS + i + 1] = w_v[i // 3, i % 3, plane : plane + 1]

    last = DEPTH - 1
    greetings = 10 + y * ((z + last - 1) // last + (2 * last - 1 - z) // last)
    wrapped = (z + last - HALF) // last + 2 * (DEPTH - HALF) * (1 - y) * ((last - z) // last)
    greetings += wrapped * (1 - (space + 7) // 8)
    pl.semaphore_wait(barrier, greetings)

    @pl.when((z == 0) & (y == 0) & (space == 0))
    def _():
        for far in range(2 * HALF, 2 * DEPTH):
            signal(token_0, {"tm": tm + far})

    def send(source, target, send_sem, recv_sem, where):
        copy = pltpu.make_async_remote_copy(
            src_ref=source, dst_ref=target, send_sem=send_sem, recv_sem=recv_sem,
            device_id=where, device_id_type=pl.DeviceIdType.MESH,
        )
        copy.start()
        return copy

    def send_part(q):
        part, k = (slice(None), q), 2 + 2 * q
        return [
            send(s_v.at[part], s_prev.at[part], near_send.at[k], near_recv.at[k], {"tm": later}),
            send(p_v.at[part], p_next.at[part], near_send.at[k + 1], near_recv.at[k + 1],
                 {"tm": earlier}),
        ]

    first_part = send_part(0)
    near = [
        send(edge_low, from_high, near_send.at[0], near_recv.at[0], {"space": below}),
        send(edge_high, from_low, near_send.at[1], near_recv.at[1], {"space": above}),
    ] + first_part + send_part(1) + send_part(2)

    @pl.when(z > 1)
    def _():
        pl.semaphore_wait(token, 1)

    def hand_up(semaphore):
        signal(semaphore, {"tm": tm + 2})
        signal(semaphore, {"tm": tm + 1})

    @pl.when((y == 1) & (z > 0) & (z < DEPTH - 1))
    def _():
        hand_up(token)

    @pl.when(z > 0)
    def _():
        pl.semaphore_wait(token_0, 1)

    @pl.when((y == 1) & ((z < HALF - 1) | ((space > 0) & (z < DEPTH - 1))))
    def _():
        hand_up(token_0)

    @pl.when(z > 0)
    def _():
        signal(ready, {"tm": at_plane(0, 0)})

    def announce(plane, carry):
        signal(ready, {"tm": at_plane(plane, 0)})
        return carry

    lax.fori_loop(1, z, announce, 0)

    cond_rows[...] = swap_blocks(cond_v[group])
    own_cond[...] = jnp.broadcast_to(cond_rows[pl.ds(rank, 1)], (LANES, LANES)).T

    row = lax.broadcasted_iota(jnp.int32, (8, LANES), 0)
    lane = lax.broadcasted_iota(jnp.int32, (8, LANES), 1)
    loads[3].wait()
    for copy in near[:2]:
        copy.wait_recv()

    def around(field, i, low, high):
        centre = field[i // 3, i % 3]
        low = jnp.broadcast_to(jnp.where(space == 0, 0.0, low), (8, LANES))
        high = jnp.broadcast_to(jnp.where(space == 7, 0.0, high), (8, LANES))
        z_low = jnp.where(row == 0, low, pltpu.roll(centre, 1, 0))
        z_high = jnp.where(row == 7, high, pltpu.roll(centre, 7, 0))
        y_low = jnp.where(lane == 0, 0.0, pltpu.roll(centre, 1, 1))
        y_high = jnp.where(lane == LANES - 1, 0.0, pltpu.roll(centre, LANES - 1, 1))
        total = (z_low + z_high) + (y_low + y_high)
        if i > 0:
            total += field[(i - 1) // 3, (i - 1) % 3]
        if i < ROWS - 1:
            total += field[(i + 1) // 3, (i + 1) % 3]
        return total

    mine = pl.ds(pl.multiple_of(2 * tm, 2), 2)

    def serve(plane, first):
        for j in (5, 4, 7, 3, 6, 2, 1, 0)[: 8 - first]:
            peer = at_plane(plane, j)
            theirs = pl.ds(pl.multiple_of(2 * peer, 2), 2)
            send(blocks.at[theirs], got.at[mine], block_send, block_recv, {"tm": peer})

    def serve_plane(plane, carry):
        serve(plane, 0)
        return carry

    def serve_lower(plane, carry):
        @pl.when(plane < z)
        def _():
            serve(plane, 0)

        return carry

    for i in range(ROWS):
        at = (i // 3, i % 3)
        s, p, w, cond = s_v[at], p_v[at], w_v[at], cond_v[i]
        around_s = around(s_v, i, from_low[i : i + 1], from_high[i : i + 1])
        around_w = around(
            w_v, i, from_low[ROWS + i : ROWS + i + 1], from_high[ROWS + i : ROWS + i + 1]
        )
        rs_ref[i] = s + diffusion * (cond * (6.0 * s - around_s)) - control_cost * p
        rp_ref[i] = p + diffusion * (6.0 * w - around_w) + tracking * (s - target_v[i])

    for q in range(3):
        for copy in near[2 + 2 * q : 4 + 2 * q]:
            copy.wait_recv()
        for i in range(q, ROWS, 3):
            rs = rs_ref[i] - s_prev[i // 3, q]
            rp = rp_ref[i] - p_next[i // 3, q]
            rs_ref[i] = rs
            rp_ref[i] = rp
            blocks[pl.ds(16 * i, 8, stride=2)] = swap_blocks(rs)
            blocks[pl.ds(16 * i + 1, 8, stride=2)] = swap_blocks(rp)
        lax.fori_loop(4 * q, 4 * q + 4, serve_lower, 0)

        @pl.when(lax.div(z, 4) == q)
        def _():
            serve(z, 1)

    own = pltpu.make_async_copy(blocks.at[mine], got.at[mine], block_recv)
    own.start()

    @pl.when(z < DEPTH - 1)
    def _():
        pl.semaphore_wait(ready, DEPTH - 1 - z)

    lax.fori_loop(z + 1, DEPTH, serve_plane, 0)
    for load in loads[4:]:
        load.wait()
    pltpu.make_async_copy(got, got, block_recv).wait()
    sent = blocks.at[pl.ds(0, TERMS - 2)]
    pltpu.make_async_copy(sent, sent, block_send).wait()
    for copy in near:
        copy.wait_send()


def solve(
    rs_ref, rp_ref, got, own_cond, high_v, low_v, trig_v,
    rs_hbm, rp_hbm, spec_hbm,
    spec_v, sem,
):
    copies = [
        pltpu.make_async_copy(rs_ref, rs_hbm, sem.at[0]),
        pltpu.make_async_copy(rp_ref, rp_hbm, sem.at[1]),
    ]
    for copy in copies:
        copy.start()
    def product(values, table):
        return lax.dot_general(
            values, table, (((0,), (0,)), ((), ())), preferred_element_type=jnp.float32
        )

    values = got[...]
    high = values.astype(jnp.bfloat16)
    low = (values - high.astype(jnp.float32)).astype(jnp.bfloat16)
    spectra = product(high, high_v[...]) + (product(high, low_v[...]) + product(low, high_v[...]))
    state_real, state_imag, adjoint_real, adjoint_imag = (
        spectra[:, LANES * i : LANES * (i + 1)] for i in range(4)
    )
    cosine, sine = trig_v[0:1], trig_v[1:2]
    diagonal = 1.0 + diffusion * 6.0 * own_cond[...] - cosine
    scale = 1.0 / (diagonal * diagonal + sine * sine + control_cost * tracking)
    fixes = (
        diagonal * state_real + sine * state_imag + control_cost * adjoint_real,
        diagonal * state_imag - sine * state_real + control_cost * adjoint_imag,
        diagonal * adjoint_real - sine * adjoint_imag - tracking * state_real,
        diagonal * adjoint_imag + sine * adjoint_real - tracking * state_imag,
    )
    for i, fix in enumerate(fixes):
        spec_v[i] = (fix * scale)[:, :STEPS]
        copy = pltpu.make_async_copy(spec_v.at[i], spec_hbm.at[i], sem.at[2 + i])
        copy.start()
        copies.append(copy)
    for copy in copies:
        copy.wait()


def shards(state_field, adjoint, target, conductivity):
    high, low, trig = dft_table()
    tiles = (ROWS, 8, LANES)
    parts = (ROWS // 3, 3, 8, LANES)
    stay = lambda array: pltpu.with_memory_space_constraint(array, pltpu.HBM)
    rows_first = lambda field: stay(jnp.transpose(field[0], (1, 0, 2)))
    in_parts = lambda field: stay(jnp.transpose(field[0], (1, 0, 2)).reshape(parts))
    vmem, dma = pltpu.VMEM, pltpu.SemaphoreType.DMA
    f32 = jnp.float32
    in_hbm = pl.BlockSpec(memory_space=pltpu.HBM)
    in_vmem = pl.BlockSpec(memory_space=pltpu.VMEM)
    rs, rp, got, own_cond, high, low, trig = pl.pallas_call(
        kernel,
        out_shape=(
            jax.ShapeDtypeStruct(tiles, f32),
            jax.ShapeDtypeStruct(tiles, f32),
            jax.ShapeDtypeStruct((TERMS, LANES), f32),
            jax.ShapeDtypeStruct((LANES, LANES), f32),
            jax.ShapeDtypeStruct((TERMS, 4 * LANES), jnp.bfloat16),
            jax.ShapeDtypeStruct((TERMS, 4 * LANES), jnp.bfloat16),
            jax.ShapeDtypeStruct((8, LANES), f32),
        ),
        in_specs=[in_hbm] * 7,
        out_specs=(in_vmem,) * 7,
        scratch_shapes=[
            vmem(parts, f32),
            vmem(parts, f32),
            vmem(parts, f32),
            vmem(tiles, f32),
            vmem(tiles, f32),
            vmem(parts, f32),
            vmem(parts, f32),
            vmem((2 * ROWS, LANES), f32),
            vmem((2 * ROWS, LANES), f32),
            vmem((2 * ROWS, LANES), f32),
            vmem((2 * ROWS, LANES), f32),
            vmem((TERMS, LANES), f32),
            vmem((8, LANES), f32),
            dma((7,)),
            dma((8,)),
            dma((8,)),
            dma,
            dma,
            pltpu.SemaphoreType.REGULAR,
            pltpu.SemaphoreType.REGULAR,
            pltpu.SemaphoreType.REGULAR,
        ],
        compiler_params=pltpu.CompilerParams(
            collective_id=0, has_side_effects=True, vmem_limit_bytes=24 * 1024 * 1024
        ),
    )(
        in_parts(state_field), in_parts(adjoint), rows_first(target),
        stay(jnp.transpose(conductivity, (1, 0, 2))),
        stay(jnp.asarray(high)), stay(jnp.asarray(low)), stay(jnp.asarray(trig)),
    )
    rs, rp, spec = pl.pallas_call(
        solve,
        out_shape=(
            jax.ShapeDtypeStruct(tiles, f32),
            jax.ShapeDtypeStruct(tiles, f32),
            jax.ShapeDtypeStruct((4, LANES, STEPS), f32),
        ),
        in_specs=[in_vmem] * 7,
        out_specs=(in_hbm,) * 3,
        scratch_shapes=[vmem((4, LANES, STEPS), f32), dma((6,))],
        compiler_params=pltpu.CompilerParams(vmem_limit_bytes=16 * 1024 * 1024),
    )(rs, rp, got, own_cond, high, low, trig)
    back = lambda tile: jnp.transpose(tile, (1, 0, 2))[None]
    spectral = jnp.transpose(spec.reshape(4, 8, BLOCK, STEPS), (0, 3, 1, 2))
    return back(rs), back(rp), spectral


def solution(mesh):
    placed = (
        P("tm", "space", None, None),
        P("tm", "space", None, None),
        P("tm", "space", None, None),
        P("space", None, None),
    )
    return jax.shard_map(
        shards,
        mesh=mesh,
        in_specs=placed,
        out_specs=(
            P("tm", "space", None, None),
            P("tm", "space", None, None),
            P(None, None, "space", "tm"),
        ),
        check_vma=False,
    )
```
